32 devices in a mesh: groups: 2 (over y), blocks: 4 (over z), dp: 2 (over x), sub: 2 (over core).
Axes of the slice: x: 2, y: 2, z: 4, core: 2. Of those that a mesh axis runs over, the one named last changes fastest.
Arguments:
- features: bfloat16 [8, 96, 2048], P(('groups', 'dp', 'sub'), None, 'blocks'), parts along dimension 0, may hold values from -6 to 6
- grad_out: bfloat16 [8, 96, 2048], P(('groups', 'dp', 'sub'), None, 'blocks'), parts along dimension 0, may hold values from -6 to 6
- weight_one: bfloat16 [96, 2592], replicated, may hold values from -0.21875 to 0.21875
- weight_two: bfloat16 [96, 2592], replicated, may hold values from -0.21875 to 0.21875
- bias_one: float32 [96], replicated, may hold values from -3 to 3
- bias_two: float32 [96], replicated, may hold values from -3 to 3
- heights: int32 [8, 16, 64], P(('groups', 'dp', 'sub'), 'blocks'), parts along dimension 0, may hold values from 2 to 4
- counts: int32 [8, 16, 64], P(('groups', 'dp', 'sub'), 'blocks'), parts along dimension 0, may hold values from 1 to 2
- neighbours: int32 [8, 16, 8], P(('groups', 'dp', 'sub'), 'blocks'), parts along dimension 0, may hold values from -1 to 15, as said below
Outputs:
- out_features: bfloat16 [8, 96, 2048], P(('groups', 'dp', 'sub'), None, 'blocks'), parts along dimension 0
- input_grad: bfloat16 [8, 96, 2048], P(('groups', 'dp', 'sub'), None, 'blocks'), parts along dimension 0
- weight_one_grad: float32 [192, 2592], P('groups'), parts along dimension 0
- weight_two_grad: float32 [192, 2592], P('groups'), parts along dimension 0
- bias_one_grad: float32 [192], P('groups'), parts along dimension 0
- bias_two_grad: float32 [192], P('groups'), parts along dimension 0
The draws below stay inside these ranges and needn't reach their ends.
There are 2 independent parts, one for each index of `groups`. The reference program is written for one: setup_inputs(seed, part) draws one part's arguments, and reference() takes and returns one part's arrays. A program takes and returns all parts, laid end to end along the dimension named above; an argument that names none is the same for every part. Nothing has to cross between parts.
Inputs may be any that keep to these rules, and one draw needn't show every extreme that they name: A global slot is the device index along blocks times 4 plus the local slot. Each region is a sheet of 4 by 4 blocks cut into tiles of 2 x 2 blocks, on a grid of 2 rows and 2 columns of tiles; a device holds one tile of each of its 1 regions (local slot 4 r + 2 i + j is block (i, j) of the tile of region r). The tile in row a and column b of a region lies on the device (start + 2 a + b) mod 4, with a start drawn for each region. The relation is symmetric and geometric, and neighbours never cross regions.
All inputs are finite; a program needn't handle non-finite values.
Results may differ from the reference program's by a relative error of at most 0.006.
Values may be sent and summed in bfloat16 or wider, within the bound.
A program may use at most 64 MiB of HBM per device.

```python
import jax
import jax.numpy as jnp
import numpy as np
from jax import lax

C = 96
SIDE = 8
KMAX = 2
RPD = 1
SLOTS = 4
SLOTS_ALL = 16
ROWS_ALL = 2048
DATA_SETS = 4
TILES_Y = 2
SHARDS = 16


DIRECTIONS = ((1, 0), (-1, 0), (0, 1), (0, -1), (1, 1), (1, -1), (-1, 1), (-1, -1))


def draw_neighbours(key, part):
    key = jax.random.fold_in(key, 7)
    tile_count = 2 * TILES_Y
    starts = jax.random.randint(key, (DATA_SETS * RPD, 1), 0, tile_count).astype(jnp.int32)
    positions = jnp.arange(tile_count, dtype=jnp.int32)[None, :]
    orders = ((positions - starts) % tile_count).astype(jnp.int32)
    holders = ((positions + starts) % tile_count).astype(jnp.int32)
    tile_row = orders // TILES_Y
    tile_col = orders % TILES_Y
    within = jnp.arange(4, dtype=jnp.int32)
    block_x = 2 * tile_row[:, :, None] + within[None, None, :] // 2
    block_y = 2 * tile_col[:, :, None] + within[None, None, :] % 2
    direction_steps = jnp.array(DIRECTIONS, jnp.int32)
    next_x = block_x[..., None] + direction_steps[:, 0]
    next_y = block_y[..., None] + direction_steps[:, 1]
    inside = (next_x >= 0) & (next_x < 4) & (next_y >= 0) & (next_y < tile_count)
    safe_x = jnp.clip(next_x, 0, 3)
    safe_y = jnp.clip(next_y, 0, tile_count - 1)
    next_tile = safe_x // 2 * TILES_Y + safe_y // 2
    stream_base = (jnp.arange(DATA_SETS * RPD, dtype=jnp.int32) * tile_count)[:, None, None, None]
    next_device = jnp.take(holders.reshape(-1), stream_base + next_tile)
    region = (jnp.arange(DATA_SETS * RPD, dtype=jnp.int32) % RPD)[:, None, None, None]
    next_slot = region * 4 + safe_x % 2 * 2 + safe_y % 2
    neighbour_ids = jnp.where(inside, next_device * SLOTS + next_slot, -1).astype(jnp.int32)
    neighbour_ids = neighbour_ids.reshape(DATA_SETS, RPD, tile_count, 4, 8).transpose(0, 2, 1, 3, 4)
    return neighbour_ids.reshape(DATA_SETS, tile_count * RPD * 4, 8)


def place_ends(entries, key, smallest, largest):
    longest = entries.shape.index(max(entries.shape))
    spots = []
    for shift in (0, 1):
        where = [jax.random.randint(jax.random.fold_in(key, axis), (), 0, length) for axis, length in enumerate(entries.shape)]
        where[longest] = (where[longest] + shift) % entries.shape[longest]
        spots.append(tuple(where))
    return entries.at[spots[0]].set(smallest).at[spots[1]].set(largest)


def steps_of(own_key, dims, split, smallest, high):
    def one(axis_at, shards_of):
        draws = jax.random.uniform(jax.random.fold_in(jax.random.fold_in(own_key, 6), axis_at), (shards_of,), jnp.float32, smallest / len(split), high / len(split))
        return jnp.repeat(jnp.exp(draws), dims[axis_at] // shards_of).reshape((-1,) + (1,) * (len(dims) - axis_at - 1))

    level = one(*split[0])
    for cut in split[1:]:
        level = level * one(*cut)
    return level


def scatter_about(stream_key, dims, spread, bound, cuts=(), kind=jnp.bfloat16):
    drawn = jax.random.normal(stream_key, dims, jnp.float32) * spread
    if len(cuts) > 0:
        drawn = steps_of(stream_key, dims, cuts, -0.22, 0.18) * drawn
    return jnp.clip(drawn, min=-bound, max=bound).astype(kind)


def setup_inputs(seed: int = 0, part: int = 0) -> dict:
    seeds = jax.random.split(jax.random.key(seed), 10)
    part_keys = jax.random.split(jax.random.fold_in(seeds[9], part), 10)
    features = scatter_about(part_keys[0], (DATA_SETS, C, ROWS_ALL), 1.0, 6.0, ((0, 4), (2, 4)))
    grad_out = scatter_about(part_keys[1], (DATA_SETS, C, ROWS_ALL), 1.0, 6.0, ((0, 4), (2, 4)))
    weight_one = scatter_about(seeds[2], (C, 27 * C), (9 * C) ** -0.5, 0.21875)
    weight_two = scatter_about(seeds[3], (C, 27 * C), (9 * C) ** -0.5, 0.21875)
    bias_one = scatter_about(seeds[4], (C,), 0.5, 3.0, (), jnp.float32)
    bias_two = scatter_about(seeds[5], (C,), 0.5, 3.0, (), jnp.float32)
    heights = place_ends(jax.random.randint(part_keys[6], (DATA_SETS, SLOTS_ALL, SIDE * SIDE), SIDE // 2 - 2, SIDE // 2 + 1), jax.random.fold_in(part_keys[6], 1), SIDE // 2 - 2, (SIDE // 2 + 1) - 1).astype(jnp.int32)
    counts = place_ends(jax.random.randint(part_keys[7], (DATA_SETS, SLOTS_ALL, SIDE * SIDE), 1, KMAX + 1), jax.random.fold_in(part_keys[7], 1), 1, KMAX).astype(jnp.int32)
    neighbours = draw_neighbours(jax.random.fold_in(jax.random.fold_in(seeds[9], part), 71), part)
    return {"features": features, "grad_out": grad_out, "weight_one": weight_one, "weight_two": weight_two, "bias_one": bias_one, "bias_two": bias_two, "heights": heights, "counts": counts, "neighbours": neighbours}


DIRECTIONS = ((1, 0), (-1, 0), (0, 1), (0, -1), (1, 1), (1, -1), (-1, 1), (-1, -1))
SHIFTS = np.array([[vertical, across, along] for vertical in (-1, 0, 1) for across in (-1, 0, 1) for along in (-1, 0, 1)], np.int32)

def silu_slope(values):
    squash = jax.nn.sigmoid(values)
    return squash * (1.0 + values * (1.0 - squash))

def grid_layout(halo_depth, side):
    direction_codes = []
    columns = []
    for grid_x in range(-halo_depth, side + halo_depth):
        for grid_y in range(-halo_depth, side + halo_depth):
            step_x = int(grid_x >= side) - int(grid_x < 0)
            step_y = int(grid_y >= side) - int(grid_y < 0)
            if step_x == 0 and step_y == 0:
                direction_codes.append(-1)
            else:
                direction_codes.append(DIRECTIONS.index((step_x, step_y)))
            columns.append((grid_x - side * step_x) * side + (grid_y - side * step_y))
    return (np.array(direction_codes, np.int32), np.array(columns, np.int32))

def conv_index(grid_heights, grid_counts, grid_ids, halo_depth, out_depth, zero_row):
    grid_width = SIDE + 2 * halo_depth
    out_width = SIDE + 2 * out_depth
    margin = halo_depth - out_depth
    spots = np.arange(out_width, dtype=np.int32) + margin
    centre = (spots[:, None] * grid_width + spots[None, :]).reshape(-1)
    source = ((spots[None, :, None] + SHIFTS[:, 1][:, None, None]) * grid_width + spots[None, None, :] + SHIFTS[:, 2][:, None, None]).reshape(27, -1)
    own_heights = grid_heights[:, centre]
    own_counts = grid_counts[:, centre]
    source_heights = grid_heights[:, source]
    source_counts = grid_counts[:, source]
    source_ids = grid_ids[:, source]
    layers = jnp.arange(KMAX, dtype=jnp.int32)[:, None, None, None]
    level_index = own_heights[None, :, None, :] + layers + SHIFTS[:, 0][None, None, :, None] - source_heights[None]
    row_live = layers < own_counts[None, :, None, :]
    present = row_live & (level_index >= 0) & (level_index < source_counts[None])
    picked = jnp.where(present, source_ids[None] * KMAX + level_index, zero_row)
    gather_index = jnp.transpose(picked, (2, 1, 3, 0)).reshape(27, -1).astype(jnp.int32)
    live_kmax = jnp.arange(KMAX, dtype=jnp.int32)[:, None, None] < own_counts[None]
    live_rows = jnp.transpose(live_kmax, (1, 2, 0)).reshape(-1)
    return (gather_index, live_rows)

def convolve(source_table, gather_index, weights):
    kernel = weights.reshape(C, C, 27).astype(jnp.float32)
    running = jnp.zeros((C, gather_index.shape[1]), jnp.float32)
    for group_number in range(3):
        gathered = jnp.take(source_table, gather_index[9 * group_number:9 * group_number + 9], axis=1).astype(jnp.float32)
        running = running + jnp.einsum('oik,ikr->or', kernel[:, :, 9 * group_number:9 * group_number + 9], gathered)
    return running

def convolve_back(source_table, gather_index, weights):
    kernel = weights.reshape(C, C, 27).astype(jnp.float32)
    flipped = gather_index[::-1]
    running = jnp.zeros((C, gather_index.shape[1]), jnp.float32)
    for group_number in range(3):
        gathered = jnp.take(source_table, flipped[9 * group_number:9 * group_number + 9], axis=1).astype(jnp.float32)
        running = running + jnp.einsum('oik,okr->ir', kernel[:, :, 9 * group_number:9 * group_number + 9], gathered)
    return running

def kernel_grad(source_table, gather_index, gradients):
    pieces = []
    for group_number in range(3):
        gathered = jnp.take(source_table, gather_index[9 * group_number:9 * group_number + 9], axis=1).astype(jnp.float32)
        pieces.append(jnp.einsum('or,ikr->oik', gradients.astype(jnp.float32), gathered))
    return jnp.concatenate(pieces, axis=2).reshape(C, C * 27)

def region_grid(region_heights, region_counts, region_neighbours):
    direction_codes, columns = grid_layout(1, SIDE)
    slot_total = region_heights.shape[0]
    own_slots = jnp.arange(slot_total, dtype=jnp.int32)[:, None]
    nearby = region_neighbours[:, np.maximum(direction_codes, 0)]
    chosen = jnp.where(direction_codes[None, :] < 0, own_slots, nearby)
    zero_column = slot_total * SIDE * SIDE
    grid_ids = jnp.where(chosen >= 0, chosen * SIDE * SIDE + columns[None, :], zero_column).astype(jnp.int32)
    zero_tail = jnp.zeros((1,), jnp.int32)
    height_table = jnp.concatenate([region_heights.reshape(-1), zero_tail])
    count_table = jnp.concatenate([region_counts.reshape(-1), zero_tail])
    return (grid_ids, height_table[grid_ids], count_table[grid_ids], zero_column)

def reference(features, grad_out, weight_one, weight_two, bias_one, bias_two, heights, counts, neighbours):
    padding = jnp.zeros((C, KMAX), jnp.bfloat16)

    def one_region(batch):
        region_rows, upstream, region_heights, region_counts, region_neighbours = batch
        grid_ids, grid_heights, grid_counts, zero_column = region_grid(region_heights, region_counts, region_neighbours)
        gather_index, live_rows = conv_index(grid_heights, grid_counts, grid_ids, 1, 0, zero_column * KMAX)
        live = live_rows[None, :]
        masked = jnp.where(live, region_rows, 0).astype(jnp.bfloat16)
        input_table = jnp.concatenate([masked, padding], axis=1)
        pre_one = convolve(input_table, gather_index, weight_one) + bias_one[:, None]
        hidden = jnp.where(live, jax.nn.silu(pre_one), 0.0).astype(jnp.bfloat16)
        hidden_table = jnp.concatenate([hidden, padding], axis=1)
        pre_two = convolve(hidden_table, gather_index, weight_two) + bias_two[:, None]
        out_features = jnp.where(live, jax.nn.silu(pre_two), 0.0).astype(jnp.bfloat16)
        grad_two = jnp.where(live, upstream.astype(jnp.float32) * silu_slope(pre_two), 0.0).astype(jnp.bfloat16)
        weight_two_part = kernel_grad(hidden_table, gather_index, grad_two)
        bias_two_part = lax.optimization_barrier(jnp.sum(grad_two.astype(jnp.float32), axis=1))
        hidden_sum = convolve_back(jnp.concatenate([grad_two, padding], axis=1), gather_index, weight_two)
        grad_one = jnp.where(live, hidden_sum * silu_slope(pre_one), 0.0).astype(jnp.bfloat16)
        weight_one_part = kernel_grad(input_table, gather_index, grad_one)
        bias_one_part = lax.optimization_barrier(jnp.sum(grad_one.astype(jnp.float32), axis=1))
        input_grad = jnp.where(live, convolve_back(jnp.concatenate([grad_one, padding], axis=1), gather_index, weight_one), 0.0).astype(jnp.bfloat16)
        return (out_features, input_grad, weight_one_part, weight_two_part, bias_one_part, bias_two_part)
    results = lax.map(one_region, (features, grad_out, heights, counts, neighbours))
    scale = 1.0 / SHARDS
    return (results[0], results[1], lax.optimization_barrier(jnp.sum(results[2], axis=0)) * scale, lax.optimization_barrier(jnp.sum(results[3], axis=0)) * scale, lax.optimization_barrier(jnp.sum(results[4], axis=0)) * scale, lax.optimization_barrier(jnp.sum(results[5], axis=0)) * scale)
```

```python
import functools

import jax
import jax.numpy as jnp
import numpy as np
from jax import lax
from jax.experimental import pallas as pl
from jax.experimental.pallas import tpu as pltpu
from jax.sharding import PartitionSpec as P

C = 96
LANES = 128
SIDE = 8
KMAX = 2
LOW = 2
LEVELS = 4
EDGE = 2 * SIDE
PLANE = EDGE * EDGE
CELLS = LEVELS * PLANE
WIDE = EDGE * (EDGE + 2)
ROWS = 4 * SIDE * SIDE * KMAX
TAPS = 27
DEPTH = TAPS * LANES
BF16 = jnp.bfloat16
F32 = jnp.float32
MESH = pl.DeviceIdType.MESH


def side_offsets(parties):
    half = parties // 2
    found = []
    for offset in (1, parties - 1, (half + 1) % parties, (half - 1) % parties):
        if offset not in found:
            found.append(offset)
    return found


def dot(left, right, dims=((1,), (0,))):
    return lax.dot_general(left, right, (dims, ((), ())), preferred_element_type=F32)


def slope_of(values):
    squash = jax.nn.sigmoid(values)
    return squash * (1.0 + values * (1.0 - squash))


def iota(shape, axis):
    return lax.broadcasted_iota(jnp.int32, shape, axis)


def one_hot(condition):
    return jnp.where(condition, 1.0, 0.0).astype(BF16)


def kernel(
    parties,
    features,
    grad_out,
    target,
    flags,
    weight_one,
    weight_two,
    bias_one,
    bias_two,
    out_features,
    input_grad,
    grad_w_one,
    grad_w_two,
    grad_b_one,
    grad_b_two,
    place,
    spread_left,
    spread_right,
    pick,
    turned,
    back,
    taps_one,
    taps_two,
    taps_back,
    pre_kept,
    mask_kept,
    send_side,
    send_across,
    got_side,
    got_across,
    send_sem,
    recv_sem,
):
    offsets = side_offsets(parties)
    half = parties // 2
    me = lax.axis_index("blocks")
    partners = offsets + [half]

    barrier = pltpu.get_barrier_semaphore()
    for offset in partners:
        pl.semaphore_signal(
            barrier, inc=1, device_id={"blocks": lax.rem(me + offset, parties)}, device_id_type=MESH
        )

    place[...] = one_hot(iota((CELLS, ROWS), 0) == target[...])
    mask_kept[...] = dot(place[...], jnp.ones((ROWS, LANES), BF16))

    row = iota((LEVELS * WIDE, LANES), 0)
    level = row // WIDE
    across = (row % WIDE) // EDGE
    along = row % EDGE
    wanted = jnp.where(
        across == 0,
        64 + level * EDGE + EDGE - 1,
        jnp.where(across == EDGE + 1, 64 + level * EDGE, level * EDGE + across - 1),
    )
    lane = iota((LEVELS * WIDE, LANES), 1)
    spread_left[...] = one_hot((along == 0) & (lane == wanted))
    spread_right[...] = one_hot((along == EDGE - 1) & (lane == wanted))
    number = iota((128, CELLS), 0)
    spot = (number % 64) * EDGE + jnp.where(number >= 64, EDGE - 1, 0)
    pick[...] = one_hot(iota((128, CELLS), 1) == spot)

    for taps in (taps_one, taps_two, taps_back):
        taps[0] = jnp.zeros((WIDE, 3 * LANES), BF16)
        taps[LEVELS + 1] = jnp.zeros((WIDE, 3 * LANES), BF16)

    def dense(rows_ref):
        padded = jnp.concatenate([rows_ref[...], jnp.zeros((LANES - C, ROWS), BF16)], axis=0)
        return dot(place[...], padded, ((1,), (1,))).astype(BF16)

    def sparse(cells):
        return dot(jnp.transpose(cells), place[...])[:C].astype(BF16)

    def copies(turn):
        result = []
        for slot, offset in enumerate(offsets):
            result.append(
                pltpu.make_async_remote_copy(
                    src_ref=send_side.at[turn],
                    dst_ref=got_side.at[turn, slot],
                    send_sem=send_sem.at[turn, slot],
                    recv_sem=recv_sem.at[turn, slot],
                    device_id={"blocks": lax.rem(me + offset, parties)},
                    device_id_type=MESH,
                )
            )
        result.append(
            pltpu.make_async_remote_copy(
                src_ref=send_across.at[turn],
                dst_ref=got_across.at[turn],
                send_sem=send_sem.at[turn, len(offsets)],
                recv_sem=recv_sem.at[turn, len(offsets)],
                device_id={"blocks": lax.rem(me + half, parties)},
                device_id_type=MESH,
            )
        )
        return result

    def send(turn, cells):
        send_side[turn] = dot(pick[...], cells).astype(BF16)
        for z in range(LEVELS):
            send_across[turn, z * EDGE : (z + 1) * EDGE] = cells[z * PLANE : z * PLANE + EDGE]
            send_across[turn, 64 + z * EDGE : 64 + (z + 1) * EDGE] = cells[
                (z + 1) * PLANE - EDGE : (z + 1) * PLANE
            ]
        for copy in copies(turn):
            copy.start()

    up = flags[0:1] > 0
    down = flags[1:2] > 0
    left = flags[2:3] > 0
    right = flags[3:4] > 0

    def arrive(turn, cells, taps):
        for copy in copies(turn):
            copy.wait()
        inside = iota((64, LANES), 0) % EDGE
        corner = ((inside == EDGE - 1) & up) | ((inside == 0) & down)

        def columns(main, diagonal, first, there):
            straight = got_side[turn, offsets.index(main), first : first + 64]
            slanted = got_side[turn, offsets.index(diagonal), first : first + 64]
            both = jnp.concatenate(
                [
                    jnp.where(there, straight.astype(F32), 0.0),
                    jnp.where(corner & there, slanted.astype(F32), 0.0),
                ],
                axis=0,
            )
            return both.astype(BF16)

        from_left = columns(1, (half + 1) % parties, 64, left)
        from_right = columns(parties - 1, (half - 1) % parties, 0, right)
        pieces = []
        for z in range(LEVELS):
            above = got_across[turn, 64 + z * EDGE : 64 + (z + 1) * EDGE].astype(F32)
            below = got_across[turn, z * EDGE : (z + 1) * EDGE].astype(F32)
            pieces.append(jnp.where(up, above, 0.0))
            pieces.append(cells[z * PLANE : (z + 1) * PLANE].astype(F32))
            pieces.append(jnp.where(down, below, 0.0))
        middle = jnp.concatenate(pieces, axis=0)
        place_along = iota((LEVELS * WIDE, LANES), 0) % EDGE
        before = jnp.where(place_along == 0, 0.0, pltpu.roll(middle, 1, 0))
        after = jnp.where(place_along == EDGE - 1, 0.0, pltpu.roll(middle, LEVELS * WIDE - 1, 0))
        before = (before + dot(spread_left[...], from_left)).astype(BF16)
        after = (after + dot(spread_right[...], from_right)).astype(BF16)
        middle = middle.astype(BF16)
        for z in range(LEVELS):
            part = slice(z * WIDE, (z + 1) * WIDE)
            taps[z + 1, :, 0:LANES] = before[part]
            taps[z + 1, :, LANES : 2 * LANES] = middle[part]
            taps[z + 1, :, 2 * LANES : 3 * LANES] = after[part]

    def convolve(taps, weights):
        results = []
        for z in range(LEVELS):
            parts = [
                taps[z + dz, dx * EDGE : dx * EDGE + PLANE] for dz in range(3) for dx in range(3)
            ]
            results.append(dot(jnp.concatenate(parts, axis=1), weights))
        return jnp.concatenate(results, axis=0)

    def weight_grad(gradient, taps, out):
        flipped = jnp.transpose(gradient)[:C]
        for dz in range(3):
            for dx in range(3):
                field = jnp.concatenate(
                    [taps[z + dz, dx * EDGE : dx * EDGE + PLANE] for z in range(LEVELS)], axis=0
                )
                first = (3 * dz + dx) * 3 * LANES
                out[:, first : first + 3 * LANES] = dot(flipped, field)

    def turn_back(weights):
        for tap in range(TAPS):
            other = TAPS - 1 - tap
            back[tap * LANES : (tap + 1) * LANES] = weights[
                :, other * LANES : (other + 1) * LANES
            ]

    live = mask_kept[...] > 0
    cells = dense(features)
    pl.semaphore_wait(barrier, len(partners))
    send(0, cells)
    turned[...] = jnp.transpose(weight_one[...])
    arrive(0, cells, taps_one)

    pre_one = convolve(taps_one, turned[...]) + bias_one[...]
    pre_kept[...] = pre_one
    hidden = jnp.where(live, pre_one * jax.nn.sigmoid(pre_one), 0.0).astype(BF16)
    send(1, hidden)
    turned[...] = jnp.transpose(weight_two[...])
    upstream = dense(grad_out)
    turn_back(weight_two)
    arrive(1, hidden, taps_two)

    pre_two = convolve(taps_two, turned[...]) + bias_two[...]
    grad_two = jnp.where(live, upstream.astype(F32) * slope_of(pre_two), 0.0).astype(BF16)
    send(2, grad_two)
    activated = jnp.where(live, pre_two * jax.nn.sigmoid(pre_two), 0.0).astype(BF16)
    out_features[...] = sparse(activated)
    weight_grad(grad_two, taps_two, grad_w_two)
    grad_b_two[...] = jnp.sum(grad_two.astype(F32), axis=0, keepdims=True)
    arrive(2, grad_two, taps_back)

    hidden_sum = convolve(taps_back, back[...])
    grad_one = jnp.where(live, hidden_sum * slope_of(pre_kept[...]), 0.0).astype(BF16)
    send(3, grad_one)
    turn_back(weight_one)
    weight_grad(grad_one, taps_one, grad_w_one)
    grad_b_one[...] = jnp.sum(grad_one.astype(F32), axis=0, keepdims=True)
    arrive(3, grad_one, taps_back)
    input_grad[...] = sparse(convolve(taps_back, back[...]).astype(BF16))


def tap_major(weights):
    kernel_taps = weights.reshape(C, C, TAPS).transpose(0, 2, 1)
    padded = jnp.pad(kernel_taps, ((0, LANES - C), (0, 0), (0, LANES - C)))
    return padded.reshape(LANES, DEPTH)


def channel_major(gradient):
    return gradient.reshape(C, TAPS, LANES)[:, :, :C].transpose(0, 2, 1).reshape(C, C * TAPS)


def on_device(
    features, grad_out, weight_one, weight_two, bias_one, bias_two, heights, counts, neighbours
):
    parties = lax.axis_size("blocks")
    sides = len(side_offsets(parties))
    block = np.arange(4)[:, None]
    column = np.arange(SIDE * SIDE)[None, :]
    cell = (SIDE * (block // 2) + column // SIDE) * EDGE + SIDE * (block % 2) + column % SIDE
    layer = np.arange(KMAX)[None, None, :]
    target = jnp.where(
        layer < counts[0][:, :, None],
        (heights[0][:, :, None] - LOW + layer) * PLANE + cell[:, :, None],
        -1,
    )
    target = target.astype(jnp.int32).reshape(1, ROWS)
    near = neighbours[0]
    flags = jnp.stack([near[0, 1], near[2, 0], near[0, 3], near[1, 2]]) >= 0
    flags = jnp.broadcast_to(jnp.pad(flags.astype(jnp.int32), (0, 4))[:, None], (8, LANES))
    bias = [jnp.pad(value, (0, LANES - C))[None] for value in (bias_one, bias_two)]
    vmem = pl.BlockSpec(memory_space=pltpu.VMEM)
    results = pl.pallas_call(
        functools.partial(kernel, parties),
        out_shape=(
            jax.ShapeDtypeStruct((C, ROWS), BF16),
            jax.ShapeDtypeStruct((C, ROWS), BF16),
            jax.ShapeDtypeStruct((C, DEPTH), F32),
            jax.ShapeDtypeStruct((C, DEPTH), F32),
            jax.ShapeDtypeStruct((1, LANES), F32),
            jax.ShapeDtypeStruct((1, LANES), F32),
        ),
        in_specs=[vmem] * 8,
        out_specs=[vmem] * 6,
        scratch_shapes=[
            pltpu.VMEM((CELLS, ROWS), BF16),
            pltpu.VMEM((LEVELS * WIDE, LANES), BF16),
            pltpu.VMEM((LEVELS * WIDE, LANES), BF16),
            pltpu.VMEM((128, CELLS), BF16),
            pltpu.VMEM((DEPTH, LANES), BF16),
            pltpu.VMEM((DEPTH, LANES), BF16),
            pltpu.VMEM((LEVELS + 2, WIDE, 3 * LANES), BF16),
            pltpu.VMEM((LEVELS + 2, WIDE, 3 * LANES), BF16),
            pltpu.VMEM((LEVELS + 2, WIDE, 3 * LANES), BF16),
            pltpu.VMEM((CELLS, LANES), F32),
            pltpu.VMEM((CELLS, LANES), F32),
            pltpu.VMEM((4, 128, LANES), BF16),
            pltpu.VMEM((4, 128, LANES), BF16),
            pltpu.VMEM((4, sides, 128, LANES), BF16),
            pltpu.VMEM((4, 128, LANES), BF16),
            pltpu.SemaphoreType.DMA((4, sides + 1)),
            pltpu.SemaphoreType.DMA((4, sides + 1)),
        ],
        compiler_params=pltpu.CompilerParams(
            collective_id=0, has_side_effects=True, vmem_limit_bytes=48 * 1024 * 1024
        ),
    )(
        features[0],
        grad_out[0],
        target,
        flags,
        tap_major(weight_one),
        tap_major(weight_two),
        bias[0],
        bias[1],
    )
    shards = parties * lax.axis_size("dp") * lax.axis_size("sub")
    summed = lax.psum(results[2:], ("blocks", "dp", "sub"))
    scale = 1.0 / shards
    return (
        results[0][None],
        results[1][None],
        channel_major(summed[0]) * scale,
        channel_major(summed[1]) * scale,
        summed[2][0, :C] * scale,
        summed[3][0, :C] * scale,
    )


def solution(mesh):
    placed = (
        P(("groups", "dp", "sub"), None, "blocks"),
        P(("groups", "dp", "sub"), None, "blocks"),
        P(),
        P(),
        P(),
        P(),
        P(("groups", "dp", "sub"), "blocks", None),
        P(("groups", "dp", "sub"), "blocks", None),
        P(("groups", "dp", "sub"), "blocks", None),
    )
    return jax.shard_map(
        on_device,
        mesh=mesh,
        in_specs=placed,
        out_specs=(
            P(("groups", "dp", "sub"), None, "blocks"),
            P(("groups", "dp", "sub"), None, "blocks"),
            P("groups", None),
            P("groups", None),
            P("groups"),
            P("groups"),
        ),
        check_vma=False,
    )
```

```python
import functools

import jax
import jax.numpy as jnp
import numpy as np
from jax import lax
from jax.experimental import pallas as pl
from jax.experimental.pallas import tpu as pltpu
from jax.sharding import PartitionSpec as P

C = 96
LANES = 128
SIDE = 8
KMAX = 2
LOW = 2
LEVELS = 4
EDGE = 2 * SIDE
PLANE = EDGE * EDGE
CELLS = LEVELS * PLANE
WIDE = EDGE * (EDGE + 2)
ROWS = 4 * SIDE * SIDE * KMAX
TAPS = 27
DEPTH = TAPS * LANES
TILES = 21
SUM_ROWS = 2048
BF16 = jnp.bfloat16
F32 = jnp.float32
MESH = pl.DeviceIdType.MESH


def side_offsets(parties):
    half = parties // 2
    found = []
    for offset in (1, parties - 1, (half + 1) % parties, (half - 1) % parties):
        if offset not in found:
            found.append(offset)
    return found


def dot(left, right, dims=((1,), (0,))):
    return lax.dot_general(left, right, (dims, ((), ())), preferred_element_type=F32)


def slope_of(values):
    squash = jax.nn.sigmoid(values)
    return squash * (1.0 + values * (1.0 - squash))


def iota(shape, axis):
    return lax.broadcasted_iota(jnp.int32, shape, axis)


def one_hot(condition):
    return jnp.where(condition, 1.0, 0.0).astype(BF16)


def kernel(
    parties,
    features,
    grad_out,
    target,
    flags,
    weight_one,
    weight_two,
    bias_one,
    bias_two,
    out_features,
    input_grad,
    sum_one,
    sum_two,
    place,
    spread_left,
    spread_right,
    pick,
    turned,
    back,
    taps_one,
    taps_two,
    taps_back,
    pre_kept,
    mask_kept,
    send_side,
    send_across,
    got_side,
    got_across,
    packed,
    part,
    part_sent,
    got_core,
    core_sum,
    core_sent,
    got_chip,
    chip_sum,
    chip_sent,
    got_line,
    total,
    send_sem,
    recv_sem,
    sum_send,
    sum_recv,
):
    offsets = side_offsets(parties)
    half = parties // 2
    me = lax.axis_index("blocks")
    chip = lax.axis_index("dp")
    core = lax.axis_index("sub")
    share = SUM_ROWS // 4 // parties
    partners = [{"blocks": lax.rem(me + offset, parties)} for offset in range(1, parties)]
    partners += [{"dp": 1 - chip}, {"sub": 1 - core}]

    barrier = pltpu.get_barrier_semaphore()
    for partner in partners:
        pl.semaphore_signal(barrier, inc=1, device_id=partner, device_id_type=MESH)

    place[...] = one_hot(iota((CELLS, ROWS), 0) == target[...])
    mask_kept[...] = dot(place[...], jnp.ones((ROWS, LANES), BF16))

    row = iota((LEVELS * WIDE, LANES), 0)
    level = row // WIDE
    across = (row % WIDE) // EDGE
    along = row % EDGE
    wanted = jnp.where(
        across == 0,
        64 + level * EDGE + EDGE - 1,
        jnp.where(across == EDGE + 1, 64 + level * EDGE, level * EDGE + across - 1),
    )
    lane = iota((LEVELS * WIDE, LANES), 1)
    spread_left[...] = one_hot((along == 0) & (lane == wanted))
    spread_right[...] = one_hot((along == EDGE - 1) & (lane == wanted))
    number = iota((128, CELLS), 0)
    spot = (number % 64) * EDGE + jnp.where(number >= 64, EDGE - 1, 0)
    pick[...] = one_hot(iota((128, CELLS), 1) == spot)

    for taps in (taps_one, taps_two, taps_back):
        taps[0] = jnp.zeros((WIDE, 3 * LANES), BF16)
        taps[LEVELS + 1] = jnp.zeros((WIDE, 3 * LANES), BF16)

    for layer in range(2):
        spare = SUM_ROWS - TILES * C
        part[layer, TILES * C :] = jnp.zeros((spare, LANES), F32)
        part_sent[layer, TILES * C :] = jnp.zeros((spare, LANES), BF16)

    def dense(rows_ref):
        padded = jnp.concatenate([rows_ref[...], jnp.zeros((LANES - C, ROWS), BF16)], axis=0)
        return dot(place[...], padded, ((1,), (1,))).astype(BF16)

    def sparse(cells):
        return dot(jnp.transpose(cells), place[...])[:C].astype(BF16)

    def copies(turn):
        result = []
        for slot, offset in enumerate(offsets):
            result.append(
                pltpu.make_async_remote_copy(
                    src_ref=send_side.at[turn],
                    dst_ref=got_side.at[turn, slot],
                    send_sem=send_sem.at[turn, slot],
                    recv_sem=recv_sem.at[turn, slot],
                    device_id={"blocks": lax.rem(me + offset, parties)},
                    device_id_type=MESH,
                )
            )
        result.append(
            pltpu.make_async_remote_copy(
                src_ref=send_across.at[turn],
                dst_ref=got_across.at[turn],
                send_sem=send_sem.at[turn, len(offsets)],
                recv_sem=recv_sem.at[turn, len(offsets)],
                device_id={"blocks": lax.rem(me + half, parties)},
                device_id_type=MESH,
            )
        )
        return result

    def send(turn, cells):
        send_side[turn] = dot(pick[...], cells).astype(BF16)
        for z in range(LEVELS):
            send_across[turn, z * EDGE : (z + 1) * EDGE] = cells[z * PLANE : z * PLANE + EDGE]
            send_across[turn, 64 + z * EDGE : 64 + (z + 1) * EDGE] = cells[
                (z + 1) * PLANE - EDGE : (z + 1) * PLANE
            ]
        for copy in copies(turn):
            copy.start()

    up = flags[0:1] > 0
    down = flags[1:2] > 0
    left = flags[2:3] > 0
    right = flags[3:4] > 0

    def arrive(turn, cells, taps):
        for copy in copies(turn):
            copy.wait()
        inside = iota((64, LANES), 0) % EDGE
        corner = ((inside == EDGE - 1) & up) | ((inside == 0) & down)

        def columns(main, diagonal, first, there):
            straight = got_side[turn, offsets.index(main), first : first + 64]
            slanted = got_side[turn, offsets.index(diagonal), first : first + 64]
            both = jnp.concatenate(
                [
                    jnp.where(there, straight.astype(F32), 0.0),
                    jnp.where(corner & there, slanted.astype(F32), 0.0),
                ],
                axis=0,
            )
            return both.astype(BF16)

        from_left = columns(1, (half + 1) % parties, 64, left)
        from_right = columns(parties - 1, (half - 1) % parties, 0, right)
        pieces = []
        for z in range(LEVELS):
            above = got_across[turn, 64 + z * EDGE : 64 + (z + 1) * EDGE].astype(F32)
            below = got_across[turn, z * EDGE : (z + 1) * EDGE].astype(F32)
            pieces.append(jnp.where(up, above, 0.0))
            pieces.append(cells[z * PLANE : (z + 1) * PLANE].astype(F32))
            pieces.append(jnp.where(down, below, 0.0))
        middle = jnp.concatenate(pieces, axis=0)
        place_along = iota((LEVELS * WIDE, LANES), 0) % EDGE
        before = jnp.where(place_along == 0, 0.0, pltpu.roll(middle, 1, 0))
        after = jnp.where(place_along == EDGE - 1, 0.0, pltpu.roll(middle, LEVELS * WIDE - 1, 0))
        before = (before + dot(spread_left[...], from_left)).astype(BF16)
        after = (after + dot(spread_right[...], from_right)).astype(BF16)
        middle = middle.astype(BF16)
        for z in range(LEVELS):
            part = slice(z * WIDE, (z + 1) * WIDE)
            taps[z + 1, :, 0:LANES] = before[part]
            taps[z + 1, :, LANES : 2 * LANES] = middle[part]
            taps[z + 1, :, 2 * LANES : 3 * LANES] = after[part]

    def convolve(taps, weights):
        results = []
        for z in range(LEVELS):
            parts = [
                taps[z + dz, dx * EDGE : dx * EDGE + PLANE] for dz in range(3) for dx in range(3)
            ]
            results.append(dot(jnp.concatenate(parts, axis=1), weights))
        return jnp.concatenate(results, axis=0)

    def weight_grad(gradient, taps, layer):
        flipped = jnp.transpose(gradient)[:C]
        for dz in range(3):
            for dx in range(3):
                field = jnp.concatenate(
                    [taps[z + dz, dx * EDGE : dx * EDGE + PLANE] for z in range(LEVELS)], axis=0
                )
                product = dot(flipped, field)
                for dy in range(3):
                    first = ((3 * dz + dx) * 3 + dy) * C
                    packed[:, first : first + C] = product[:, dy * LANES : dy * LANES + C]
        bias = dot(flipped, jnp.ones((CELLS, LANES), BF16))
        packed[:, TAPS * C : (TAPS + 1) * C] = bias[:, :C]
        for tile in range(TILES):
            piece = packed[:, tile * LANES : (tile + 1) * LANES]
            part[layer, tile * C : (tile + 1) * C] = piece
            part_sent[layer, tile * C : (tile + 1) * C] = piece.astype(BF16)

    half_rows, quarter = SUM_ROWS // 2, SUM_ROWS // 4
    mine = core * half_rows + chip * quarter

    def remote(source, landing, layer, number, partner):
        return pltpu.make_async_remote_copy(
            src_ref=source,
            dst_ref=landing,
            send_sem=sum_send.at[layer, number],
            recv_sem=sum_recv.at[layer, number],
            device_id=partner,
            device_id_type=MESH,
        )

    def over_cores(layer):
        other = pl.ds(pl.multiple_of((1 - core) * half_rows, 16), half_rows)
        return [
            remote(part_sent.at[layer, other], got_core.at[layer], layer, 0, {"sub": 1 - core})
        ]

    def over_chips(layer):
        other = pl.ds(pl.multiple_of((1 - chip) * quarter, 16), quarter)
        return [
            remote(core_sent.at[layer, other], got_chip.at[layer], layer, 1, {"dp": 1 - chip})
        ]

    def over_line(layer):
        result = []
        for offset in range(1, parties):
            there = lax.rem(me + offset, parties)
            rows = pl.ds(pl.multiple_of(there * share, 16), share)
            result.append(
                remote(
                    chip_sent.at[layer, rows],
                    got_line.at[layer, offset - 1],
                    layer,
                    1 + offset,
                    {"blocks": there},
                )
            )
        return result

    def spread_line(layer):
        rows = total.at[layer, pl.ds(pl.multiple_of(mine + me * share, 16), share)]
        return [
            remote(rows, rows, layer, parties + offset, {"blocks": lax.rem(me + offset, parties)})
            for offset in range(1, parties)
        ]

    def spread_chips(layer):
        rows = total.at[layer, pl.ds(pl.multiple_of(mine, 16), quarter)]
        return [remote(rows, rows, layer, 2 * parties, {"dp": 1 - chip})]

    def spread_cores(layer):
        rows = total.at[layer, pl.ds(pl.multiple_of(core * half_rows, 16), half_rows)]
        return [remote(rows, rows, layer, 2 * parties + 1, {"sub": 1 - core})]

    def begin(copies_of, layer):
        for copy in copies_of(layer):
            copy.start()

    def finish(copies_of, layer):
        for copy in copies_of(layer):
            copy.wait()

    def sum_cores(layer):
        finish(over_cores, layer)
        own = part[layer, pl.ds(pl.multiple_of(core * half_rows, 16), half_rows)]
        value = own + got_core[layer].astype(F32)
        core_sum[layer] = value
        core_sent[layer] = value.astype(BF16)
        begin(over_chips, layer)

    def sum_chips(layer):
        finish(over_chips, layer)
        own = core_sum[layer, pl.ds(pl.multiple_of(chip * quarter, 16), quarter)]
        value = own + got_chip[layer].astype(F32)
        chip_sum[layer] = value
        chip_sent[layer] = value.astype(BF16)
        begin(over_line, layer)

    def sum_line(layer):
        finish(over_line, layer)
        value = chip_sum[layer, pl.ds(pl.multiple_of(me * share, 16), share)]
        for offset in range(1, parties):
            value = value + got_line[layer, offset - 1].astype(F32)
        value = value * (1.0 / (4 * parties))
        total[layer, pl.ds(pl.multiple_of(mine + me * share, 16), share)] = value.astype(BF16)
        begin(spread_line, layer)

    def turn_back(weights):
        for tap in range(TAPS):
            other = TAPS - 1 - tap
            back[tap * LANES : (tap + 1) * LANES] = weights[
                :, other * LANES : (other + 1) * LANES
            ]

    live = mask_kept[...] > 0
    cells = dense(features)
    pl.semaphore_wait(barrier, len(partners))
    send(0, cells)
    turned[...] = jnp.transpose(weight_one[...])
    arrive(0, cells, taps_one)

    pre_one = convolve(taps_one, turned[...]) + bias_one[...]
    pre_kept[...] = pre_one
    hidden = jnp.where(live, pre_one * jax.nn.sigmoid(pre_one), 0.0).astype(BF16)
    send(1, hidden)
    turned[...] = jnp.transpose(weight_two[...])
    upstream = dense(grad_out)
    turn_back(weight_two)
    arrive(1, hidden, taps_two)

    pre_two = convolve(taps_two, turned[...]) + bias_two[...]
    grad_two = jnp.where(live, upstream.astype(F32) * slope_of(pre_two), 0.0).astype(BF16)
    send(2, grad_two)
    activated = jnp.where(live, pre_two * jax.nn.sigmoid(pre_two), 0.0).astype(BF16)
    out_features[...] = sparse(activated)
    weight_grad(grad_two, taps_two, 0)
    begin(over_cores, 0)
    arrive(2, grad_two, taps_back)
    sum_cores(0)

    hidden_sum = convolve(taps_back, back[...])
    grad_one = jnp.where(live, hidden_sum * slope_of(pre_kept[...]), 0.0).astype(BF16)
    send(3, grad_one)
    sum_chips(0)
    turn_back(weight_one)
    weight_grad(grad_one, taps_one, 1)
    begin(over_cores, 1)
    sum_line(0)
    sum_cores(1)
    arrive(3, grad_one, taps_back)
    finish(spread_line, 0)
    begin(spread_chips, 0)
    sum_chips(1)
    result = convolve(taps_back, back[...]).astype(BF16)
    finish(spread_chips, 0)
    begin(spread_cores, 0)
    sum_line(1)
    input_grad[...] = sparse(result)
    finish(spread_line, 1)
    begin(spread_chips, 1)
    finish(spread_cores, 0)
    sum_two[...] = total[0]
    finish(spread_chips, 1)
    begin(spread_cores, 1)
    finish(spread_cores, 1)
    sum_one[...] = total[1]


def tap_major(weights):
    kernel_taps = weights.reshape(C, C, TAPS).transpose(0, 2, 1)
    padded = jnp.pad(kernel_taps, ((0, LANES - C), (0, 0), (0, LANES - C)))
    return padded.reshape(LANES, DEPTH)


def channel_major(total):
    tiles = total[: TILES * C].reshape(TILES, C, LANES).transpose(1, 0, 2).reshape(C, TILES * LANES)
    kernel_grad = tiles[:, : C * TAPS].reshape(C, TAPS, C).transpose(0, 2, 1).reshape(C, C * TAPS)
    return kernel_grad.astype(F32), tiles[:, C * TAPS].astype(F32)


def on_device(
    features, grad_out, weight_one, weight_two, bias_one, bias_two, heights, counts, neighbours
):
    parties = lax.axis_size("blocks")
    sides = len(side_offsets(parties))
    block = np.arange(4)[:, None]
    column = np.arange(SIDE * SIDE)[None, :]
    cell = (SIDE * (block // 2) + column // SIDE) * EDGE + SIDE * (block % 2) + column % SIDE
    layer = np.arange(KMAX)[None, None, :]
    target = jnp.where(
        layer < counts[0][:, :, None],
        (heights[0][:, :, None] - LOW + layer) * PLANE + cell[:, :, None],
        -1,
    )
    target = target.astype(jnp.int32).reshape(1, ROWS)
    near = neighbours[0]
    flags = jnp.stack([near[0, 1], near[2, 0], near[0, 3], near[1, 2]]) >= 0
    flags = jnp.broadcast_to(jnp.pad(flags.astype(jnp.int32), (0, 4))[:, None], (8, LANES))
    bias = [jnp.pad(value, (0, LANES - C))[None] for value in (bias_one, bias_two)]
    vmem = pl.BlockSpec(memory_space=pltpu.VMEM)
    results = pl.pallas_call(
        functools.partial(kernel, parties),
        out_shape=(
            jax.ShapeDtypeStruct((C, ROWS), BF16),
            jax.ShapeDtypeStruct((C, ROWS), BF16),
            jax.ShapeDtypeStruct((SUM_ROWS, LANES), BF16),
            jax.ShapeDtypeStruct((SUM_ROWS, LANES), BF16),
        ),
        in_specs=[vmem] * 8,
        out_specs=[vmem] * 4,
        scratch_shapes=[
            pltpu.VMEM((CELLS, ROWS), BF16),
            pltpu.VMEM((LEVELS * WIDE, LANES), BF16),
            pltpu.VMEM((LEVELS * WIDE, LANES), BF16),
            pltpu.VMEM((128, CELLS), BF16),
            pltpu.VMEM((DEPTH, LANES), BF16),
            pltpu.VMEM((DEPTH, LANES), BF16),
            pltpu.VMEM((LEVELS + 2, WIDE, 3 * LANES), BF16),
            pltpu.VMEM((LEVELS + 2, WIDE, 3 * LANES), BF16),
            pltpu.VMEM((LEVELS + 2, WIDE, 3 * LANES), BF16),
            pltpu.VMEM((CELLS, LANES), F32),
            pltpu.VMEM((CELLS, LANES), F32),
            pltpu.VMEM((4, 128, LANES), BF16),
            pltpu.VMEM((4, 128, LANES), BF16),
            pltpu.VMEM((4, sides, 128, LANES), BF16),
            pltpu.VMEM((4, 128, LANES), BF16),
            pltpu.VMEM((C, TILES * LANES), F32),
            pltpu.VMEM((2, SUM_ROWS, LANES), F32),
            pltpu.VMEM((2, SUM_ROWS, LANES), BF16),
            pltpu.VMEM((2, SUM_ROWS // 2, LANES), BF16),
            pltpu.VMEM((2, SUM_ROWS // 2, LANES), F32),
            pltpu.VMEM((2, SUM_ROWS // 2, LANES), BF16),
            pltpu.VMEM((2, SUM_ROWS // 4, LANES), BF16),
            pltpu.VMEM((2, SUM_ROWS // 4, LANES), F32),
            pltpu.VMEM((2, SUM_ROWS // 4, LANES), BF16),
            pltpu.VMEM((2, parties - 1, SUM_ROWS // 4 // parties, LANES), BF16),
            pltpu.VMEM((2, SUM_ROWS, LANES), BF16),
            pltpu.SemaphoreType.DMA((4, sides + 1)),
            pltpu.SemaphoreType.DMA((4, sides + 1)),
            pltpu.SemaphoreType.DMA((2, 2 * parties + 2)),
            pltpu.SemaphoreType.DMA((2, 2 * parties + 2)),
        ],
        compiler_params=pltpu.CompilerParams(
            collective_id=0, has_side_effects=True, vmem_limit_bytes=48 * 1024 * 1024
        ),
    )(
        features[0],
        grad_out[0],
        target,
        flags,
        tap_major(weight_one),
        tap_major(weight_two),
        bias[0],
        bias[1],
    )
    weight_one_grad, bias_one_grad = channel_major(results[2])
    weight_two_grad, bias_two_grad = channel_major(results[3])
    return (
        results[0][None],
        results[1][None],
        weight_one_grad,
        weight_two_grad,
        bias_one_grad,
        bias_two_grad,
    )


def solution(mesh):
    placed = (
        P(("groups", "dp", "sub"), None, "blocks"),
        P(("groups", "dp", "sub"), None, "blocks"),
        P(),
        P(),
        P(),
        P(),
        P(("groups", "dp", "sub"), "blocks", None),
        P(("groups", "dp", "sub"), "blocks", None),
        P(("groups", "dp", "sub"), "blocks", None),
    )
    return jax.shard_map(
        on_device,
        mesh=mesh,
        in_specs=placed,
        out_specs=(
            P(("groups", "dp", "sub"), None, "blocks"),
            P(("groups", "dp", "sub"), None, "blocks"),
            P("groups", None),
            P("groups", None),
            P("groups"),
            P("groups"),
        ),
        check_vma=False,
    )
```

```python
import functools

import jax
import jax.numpy as jnp
from jax import lax
from jax.experimental import pallas as pl
from jax.experimental.pallas import tpu as pltpu
from jax.sharding import PartitionSpec as P

C = 96
LANES = 128
SIDE = 8
KMAX = 2
LOW = 2
LEVELS = 4
EDGE = 2 * SIDE
PLANE = EDGE * EDGE
CELLS = LEVELS * PLANE
WIDE = EDGE * (EDGE + 2)
ROWS = 4 * SIDE * SIDE * KMAX
TAPS = 27
DEPTH = TAPS * LANES
TILES = 21
SUM_ROWS = 2048
BF16 = jnp.bfloat16
F32 = jnp.float32
MESH = pl.DeviceIdType.MESH


def side_offsets(parties):
    half = parties // 2
    found = []
    for offset in (1, parties - 1, (half + 1) % parties, (half - 1) % parties):
        if offset not in found:
            found.append(offset)
    return found


def dot(left, right, dims=((1,), (0,))):
    return lax.dot_general(left, right, (dims, ((), ())), preferred_element_type=F32)


def slope_of(values):
    squash = jax.nn.sigmoid(values)
    return squash * (1.0 + values * (1.0 - squash))


def iota(shape, axis):
    return lax.broadcasted_iota(jnp.int32, shape, axis)


def one_hot(condition):
    return jnp.where(condition, 1.0, 0.0).astype(BF16)


def kernel(
    parties,
    features,
    grad_out,
    weight_one,
    weight_two,
    bias_one,
    bias_two,
    heights,
    counts,
    neighbours,
    out_features,
    input_grad,
    weight_one_grad,
    weight_two_grad,
    bias_one_grad,
    bias_two_grad,
    place,
    spread_left,
    spread_right,
    pick,
    square,
    strided,
    taken_one,
    taken_two,
    bias_kept,
    back,
    taps_one,
    taps_two,
    taps_back,
    pre_kept,
    mask_kept,
    send_side,
    send_across,
    got_side,
    got_across,
    part,
    part_sent,
    got_core,
    core_sum,
    core_sent,
    got_chip,
    chip_sum,
    chip_sent,
    got_line,
    total,
    send_sem,
    recv_sem,
    sum_send,
    sum_recv,
):
    offsets = side_offsets(parties)
    half = parties // 2
    me = lax.axis_index("blocks")
    chip = lax.axis_index("dp")
    core = lax.axis_index("sub")
    share = SUM_ROWS // 4 // parties
    partners = [{"blocks": lax.rem(me + offset, parties)} for offset in range(1, parties)]
    partners += [{"dp": 1 - chip}, {"sub": 1 - core}]

    barrier = pltpu.get_barrier_semaphore()
    for partner in partners:
        pl.semaphore_signal(barrier, inc=1, device_id=partner, device_id_type=MESH)

    lane = iota((SIDE * SIDE, LANES), 1)
    double = one_hot(lane // KMAX == iota((SIDE * SIDE, LANES), 0))
    low = dot(heights[0].astype(F32).astype(BF16), double).astype(jnp.int32)
    held = dot(counts[0].astype(F32).astype(BF16), double).astype(jnp.int32)
    lane = iota((1, LANES), 1)
    column = lane // KMAX
    layer = lane % KMAX
    cell_at = iota((CELLS, LANES), 0)
    for slot in range(4):
        cell = (SIDE * (slot // 2) + column // SIDE) * EDGE + SIDE * (slot % 2) + column % SIDE
        target = (low[slot : slot + 1] - LOW + layer) * PLANE + cell
        target = jnp.where(layer < held[slot : slot + 1], target, -1)
        place[:, slot * LANES : (slot + 1) * LANES] = one_hot(cell_at == target)
    mask_kept[...] = dot(place[...], jnp.ones((ROWS, LANES), BF16))

    row = iota((LEVELS * WIDE, LANES), 0)
    level = row // WIDE
    across = (row % WIDE) // EDGE
    along = row % EDGE
    wanted = jnp.where(
        across == 0,
        64 + level * EDGE + EDGE - 1,
        jnp.where(across == EDGE + 1, 64 + level * EDGE, level * EDGE + across - 1),
    )
    lane = iota((LEVELS * WIDE, LANES), 1)
    spread_left[...] = one_hot((along == 0) & (lane == wanted))
    spread_right[...] = one_hot((along == EDGE - 1) & (lane == wanted))
    number = iota((128, CELLS), 0)
    spot = (number % 64) * EDGE + jnp.where(number >= 64, EDGE - 1, 0)
    pick[...] = one_hot(iota((128, CELLS), 1) == spot)

    for taps in (taps_one, taps_two, taps_back):
        taps[0] = jnp.zeros((WIDE, 3 * LANES), BF16)
        taps[LEVELS + 1] = jnp.zeros((WIDE, 3 * LANES), BF16)

    for layer in range(2):
        spare = SUM_ROWS - TILES * C
        part[layer, TILES * C :] = jnp.zeros((spare, LANES), F32)
        part_sent[layer, TILES * C :] = jnp.zeros((spare, LANES), BF16)

    def dense(rows_ref):
        padded = jnp.concatenate([rows_ref[0], jnp.zeros((LANES - C, ROWS), BF16)], axis=0)
        return dot(place[...], padded, ((1,), (1,))).astype(BF16)

    def sparse(cells):
        return dot(jnp.transpose(cells), place[...])[:C].astype(BF16)

    def copies(turn):
        result = []
        for slot, offset in enumerate(offsets):
            result.append(
                pltpu.make_async_remote_copy(
                    src_ref=send_side.at[turn],
                    dst_ref=got_side.at[turn, slot],
                    send_sem=send_sem.at[turn, slot],
                    recv_sem=recv_sem.at[turn, slot],
                    device_id={"blocks": lax.rem(me + offset, parties)},
                    device_id_type=MESH,
                )
            )
        result.append(
            pltpu.make_async_remote_copy(
                src_ref=send_across.at[turn],
                dst_ref=got_across.at[turn],
                send_sem=send_sem.at[turn, len(offsets)],
                recv_sem=recv_sem.at[turn, len(offsets)],
                device_id={"blocks": lax.rem(me + half, parties)},
                device_id_type=MESH,
            )
        )
        return result

    def send(turn, cells):
        send_side[turn] = dot(pick[...], cells).astype(BF16)
        for z in range(LEVELS):
            send_across[turn, z * EDGE : (z + 1) * EDGE] = cells[z * PLANE : z * PLANE + EDGE]
            send_across[turn, 64 + z * EDGE : 64 + (z + 1) * EDGE] = cells[
                (z + 1) * PLANE - EDGE : (z + 1) * PLANE
            ]
        for copy in copies(turn):
            copy.start()

    def there(slot, direction):
        return jnp.broadcast_to(neighbours[0, slot : slot + 1, direction : direction + 1], (1, LANES)) >= 0

    up, down, left, right = there(0, 1), there(2, 0), there(0, 3), there(1, 2)

    def arrive(turn, cells, taps):
        for copy in copies(turn):
            copy.wait()
        inside = iota((64, LANES), 0) % EDGE
        corner = ((inside == EDGE - 1) & up) | ((inside == 0) & down)

        def columns(main, diagonal, first, there):
            straight = got_side[turn, offsets.index(main), first : first + 64]
            slanted = got_side[turn, offsets.index(diagonal), first : first + 64]
            both = jnp.concatenate(
                [
                    jnp.where(there, straight.astype(F32), 0.0),
                    jnp.where(corner & there, slanted.astype(F32), 0.0),
                ],
                axis=0,
            )
            return both.astype(BF16)

        from_left = columns(1, (half + 1) % parties, 64, left)
        from_right = columns(parties - 1, (half - 1) % parties, 0, right)
        pieces = []
        for z in range(LEVELS):
            above = got_across[turn, 64 + z * EDGE : 64 + (z + 1) * EDGE].astype(F32)
            below = got_across[turn, z * EDGE : (z + 1) * EDGE].astype(F32)
            pieces.append(jnp.where(up, above, 0.0))
            pieces.append(cells[z * PLANE : (z + 1) * PLANE].astype(F32))
            pieces.append(jnp.where(down, below, 0.0))
        middle = jnp.concatenate(pieces, axis=0)
        place_along = iota((LEVELS * WIDE, LANES), 0) % EDGE
        before = jnp.where(place_along == 0, 0.0, pltpu.roll(middle, 1, 0))
        after = jnp.where(place_along == EDGE - 1, 0.0, pltpu.roll(middle, LEVELS * WIDE - 1, 0))
        before = (before + dot(spread_left[...], from_left)).astype(BF16)
        after = (after + dot(spread_right[...], from_right)).astype(BF16)
        middle = middle.astype(BF16)
        for z in range(LEVELS):
            part = slice(z * WIDE, (z + 1) * WIDE)
            taps[z + 1, :, 0:LANES] = before[part]
            taps[z + 1, :, LANES : 2 * LANES] = middle[part]
            taps[z + 1, :, 2 * LANES : 3 * LANES] = after[part]

    def convolve(taps, weights):
        results = []
        for z in range(LEVELS):
            parts = [
                taps[z + dz, dx * EDGE : dx * EDGE + PLANE] for dz in range(3) for dx in range(3)
            ]
            results.append(dot(jnp.concatenate(parts, axis=1), weights))
        return jnp.concatenate(results, axis=0)

    def weight_grad(gradient, taps, layer):
        flipped = jnp.transpose(gradient)
        for dz in range(3):
            for dx in range(3):
                field = jnp.concatenate(
                    [taps[z + dz, dx * EDGE : dx * EDGE + PLANE] for z in range(LEVELS)], axis=0
                )
                product = jnp.transpose(dot(flipped, field))
                for dy in range(3):
                    tap = (3 * dz + dx) * 3 + dy
                    strided[pl.ds(tap, C, stride=TAPS), :] = product[dy * LANES : dy * LANES + C]
        bias = jnp.sum(gradient.astype(F32), axis=0, keepdims=True)
        strided[TAPS * C :] = jnp.broadcast_to(bias, (C, LANES))
        for tile in range(TILES):
            piece = jnp.transpose(strided[tile * LANES : (tile + 1) * LANES])[:C]
            part[layer, tile * C : (tile + 1) * C] = piece
            part_sent[layer, tile * C : (tile + 1) * C] = piece.astype(BF16)

    half_rows, quarter = SUM_ROWS // 2, SUM_ROWS // 4
    mine = core * half_rows + chip * quarter

    def remote(source, landing, layer, number, partner):
        return pltpu.make_async_remote_copy(
            src_ref=source,
            dst_ref=landing,
            send_sem=sum_send.at[layer, number],
            recv_sem=sum_recv.at[layer, number],
            device_id=partner,
            device_id_type=MESH,
        )

    def over_cores(layer):
        other = pl.ds(pl.multiple_of((1 - core) * half_rows, 16), half_rows)
        return [
            remote(part_sent.at[layer, other], got_core.at[layer], layer, 0, {"sub": 1 - core})
        ]

    def over_chips(layer):
        other = pl.ds(pl.multiple_of((1 - chip) * quarter, 16), quarter)
        return [
            remote(core_sent.at[layer, other], got_chip.at[layer], layer, 1, {"dp": 1 - chip})
        ]

    def over_line(layer):
        result = []
        for offset in range(1, parties):
            there = lax.rem(me + offset, parties)
            rows = pl.ds(pl.multiple_of(there * share, 16), share)
            result.append(
                remote(
                    chip_sent.at[layer, rows],
                    got_line.at[layer, offset - 1],
                    layer,
                    1 + offset,
                    {"blocks": there},
                )
            )
        return result

    def spread_line(layer):
        rows = total.at[layer, pl.ds(pl.multiple_of(mine + me * share, 16), share)]
        return [
            remote(rows, rows, layer, parties + offset, {"blocks": lax.rem(me + offset, parties)})
            for offset in range(1, parties)
        ]

    def spread_chips(layer):
        rows = total.at[layer, pl.ds(pl.multiple_of(mine, 16), quarter)]
        return [remote(rows, rows, layer, 2 * parties, {"dp": 1 - chip})]

    def spread_cores(layer):
        rows = total.at[layer, pl.ds(pl.multiple_of(core * half_rows, 16), half_rows)]
        return [remote(rows, rows, layer, 2 * parties + 1, {"sub": 1 - core})]

    def begin(copies_of, layer):
        for copy in copies_of(layer):
            copy.start()

    def finish(copies_of, layer):
        for copy in copies_of(layer):
            copy.wait()

    def sum_cores(layer):
        finish(over_cores, layer)
        own = part[layer, pl.ds(pl.multiple_of(core * half_rows, 16), half_rows)]
        value = own + got_core[layer].astype(F32)
        core_sum[layer] = value
        core_sent[layer] = value.astype(BF16)
        begin(over_chips, layer)

    def sum_chips(layer):
        finish(over_chips, layer)
        own = core_sum[layer, pl.ds(pl.multiple_of(chip * quarter, 16), quarter)]
        value = own + got_chip[layer].astype(F32)
        chip_sum[layer] = value
        chip_sent[layer] = value.astype(BF16)
        begin(over_line, layer)

    def sum_line(layer):
        finish(over_line, layer)
        value = chip_sum[layer, pl.ds(pl.multiple_of(me * share, 16), share)]
        for offset in range(1, parties):
            value = value + got_line[layer, offset - 1].astype(F32)
        value = value * (1.0 / (4 * parties))
        total[layer, pl.ds(pl.multiple_of(mine + me * share, 16), share)] = value.astype(BF16)
        begin(spread_line, layer)

    def take_taps(weights, taken):
        square[:C, : TAPS * C] = weights[...].astype(F32)
        for tile in range(TILES):
            part_of = slice(tile * LANES, (tile + 1) * LANES)
            strided[part_of] = jnp.transpose(square[:, part_of])
        for tap in range(TAPS):
            rows = strided[pl.ds(tap, C, stride=TAPS), :]
            taken[tap * LANES : tap * LANES + C] = rows.astype(BF16)
            taken[tap * LANES + C : (tap + 1) * LANES] = jnp.zeros((LANES - C, LANES), BF16)

    def turn_back(taken):
        for tap in range(TAPS):
            other = TAPS - 1 - tap
            tile = taken[other * LANES : (other + 1) * LANES]
            back[tap * LANES : (tap + 1) * LANES] = jnp.transpose(tile)

    def hand_out(layer, weights_out, bias_out):
        for tile in range(TILES - 1):
            piece = total[layer, tile * C : (tile + 1) * C]
            weights_out[:, tile * LANES : (tile + 1) * LANES] = piece.astype(F32)
        last = total[layer, (TILES - 1) * C :].astype(F32)
        rest = TAPS * C - (TILES - 1) * LANES
        weights_out[:, (TILES - 1) * LANES :] = last[:C, :rest]
        bias_out[...] = jnp.transpose(last)[rest : rest + 1, :C]

    square[...] = jnp.zeros((LANES, TILES * LANES), F32)
    bias_kept[...] = jnp.zeros((2, 1, LANES), F32)
    bias_kept[0, :, :C] = bias_one[...]
    bias_kept[1, :, :C] = bias_two[...]
    live = mask_kept[...] > 0
    cells = dense(features)
    pl.semaphore_wait(barrier, len(partners))
    send(0, cells)
    take_taps(weight_one, taken_one)
    arrive(0, cells, taps_one)

    pre_one = convolve(taps_one, taken_one[...]) + bias_kept[0]
    pre_kept[...] = pre_one
    hidden = jnp.where(live, pre_one * jax.nn.sigmoid(pre_one), 0.0).astype(BF16)
    send(1, hidden)
    take_taps(weight_two, taken_two)
    upstream = dense(grad_out)
    turn_back(taken_two)
    arrive(1, hidden, taps_two)

    pre_two = convolve(taps_two, taken_two[...]) + bias_kept[1]
    grad_two = jnp.where(live, upstream.astype(F32) * slope_of(pre_two), 0.0).astype(BF16)
    send(2, grad_two)
    activated = jnp.where(live, pre_two * jax.nn.sigmoid(pre_two), 0.0).astype(BF16)
    out_features[0] = sparse(activated)
    weight_grad(grad_two, taps_two, 0)
    begin(over_cores, 0)
    arrive(2, grad_two, taps_back)
    sum_cores(0)

    hidden_sum = convolve(taps_back, back[...])
    grad_one = jnp.where(live, hidden_sum * slope_of(pre_kept[...]), 0.0).astype(BF16)
    send(3, grad_one)
    sum_chips(0)
    turn_back(taken_one)
    weight_grad(grad_one, taps_one, 1)
    begin(over_cores, 1)
    sum_line(0)
    sum_cores(1)
    arrive(3, grad_one, taps_back)
    finish(spread_line, 0)
    begin(spread_chips, 0)
    sum_chips(1)
    result = convolve(taps_back, back[...]).astype(BF16)
    finish(spread_chips, 0)
    begin(spread_cores, 0)
    sum_line(1)
    input_grad[0] = sparse(result)
    finish(spread_line, 1)
    begin(spread_chips, 1)
    finish(spread_cores, 0)
    hand_out(0, weight_two_grad, bias_two_grad)
    finish(spread_chips, 1)
    begin(spread_cores, 1)
    finish(spread_cores, 1)
    hand_out(1, weight_one_grad, bias_one_grad)


def on_device(
    features, grad_out, weight_one, weight_two, bias_one, bias_two, heights, counts, neighbours
):
    parties = lax.axis_size("blocks")
    sides = len(side_offsets(parties))
    vmem = pl.BlockSpec(memory_space=pltpu.VMEM)
    results = pl.pallas_call(
        functools.partial(kernel, parties),
        out_shape=(
            jax.ShapeDtypeStruct((1, C, ROWS), BF16),
            jax.ShapeDtypeStruct((1, C, ROWS), BF16),
            jax.ShapeDtypeStruct((C, TAPS * C), F32),
            jax.ShapeDtypeStruct((C, TAPS * C), F32),
            jax.ShapeDtypeStruct((1, C), F32),
            jax.ShapeDtypeStruct((1, C), F32),
        ),
        in_specs=[vmem] * 9,
        out_specs=[vmem] * 6,
        scratch_shapes=[
            pltpu.VMEM((CELLS, ROWS), BF16),
            pltpu.VMEM((LEVELS * WIDE, LANES), BF16),
            pltpu.VMEM((LEVELS * WIDE, LANES), BF16),
            pltpu.VMEM((128, CELLS), BF16),
            pltpu.VMEM((LANES, TILES * LANES), F32),
            pltpu.VMEM((TILES * LANES, LANES), F32),
            pltpu.VMEM((DEPTH, LANES), BF16),
            pltpu.VMEM((DEPTH, LANES), BF16),
            pltpu.VMEM((2, 1, LANES), F32),
            pltpu.VMEM((DEPTH, LANES), BF16),
            pltpu.VMEM((LEVELS + 2, WIDE, 3 * LANES), BF16),
            pltpu.VMEM((LEVELS + 2, WIDE, 3 * LANES), BF16),
            pltpu.VMEM((LEVELS + 2, WIDE, 3 * LANES), BF16),
            pltpu.VMEM((CELLS, LANES), F32),
            pltpu.VMEM((CELLS, LANES), F32),
            pltpu.VMEM((4, 128, LANES), BF16),
            pltpu.VMEM((4, 128, LANES), BF16),
            pltpu.VMEM((4, sides, 128, LANES), BF16),
            pltpu.VMEM((4, 128, LANES), BF16),
            pltpu.VMEM((2, SUM_ROWS, LANES), F32),
            pltpu.VMEM((2, SUM_ROWS, LANES), BF16),
            pltpu.VMEM((2, SUM_ROWS // 2, LANES), BF16),
            pltpu.VMEM((2, SUM_ROWS // 2, LANES), F32),
            pltpu.VMEM((2, SUM_ROWS // 2, LANES), BF16),
            pltpu.VMEM((2, SUM_ROWS // 4, LANES), BF16),
            pltpu.VMEM((2, SUM_ROWS // 4, LANES), F32),
            pltpu.VMEM((2, SUM_ROWS // 4, LANES), BF16),
            pltpu.VMEM((2, parties - 1, SUM_ROWS // 4 // parties, LANES), BF16),
            pltpu.VMEM((2, SUM_ROWS, LANES), BF16),
            pltpu.SemaphoreType.DMA((4, sides + 1)),
            pltpu.SemaphoreType.DMA((4, sides + 1)),
            pltpu.SemaphoreType.DMA((2, 2 * parties + 2)),
            pltpu.SemaphoreType.DMA((2, 2 * parties + 2)),
        ],
        compiler_params=pltpu.CompilerParams(
            collective_id=0, has_side_effects=True, vmem_limit_bytes=48 * 1024 * 1024
        ),
    )(
        features,
        grad_out,
        weight_one,
        weight_two,
        bias_one[None],
        bias_two[None],
        heights,
        counts,
        neighbours,
    )
    return (*results[:4], results[4][0], results[5][0])


def solution(mesh):
    placed = (
        P(("groups", "dp", "sub"), None, "blocks"),
        P(("groups", "dp", "sub"), None, "blocks"),
        P(),
        P(),
        P(),
        P(),
        P(("groups", "dp", "sub"), "blocks", None),
        P(("groups", "dp", "sub"), "blocks", None),
        P(("groups", "dp", "sub"), "blocks", None),
    )
    return jax.shard_map(
        on_device,
        mesh=mesh,
        in_specs=placed,
        out_specs=(
            P(("groups", "dp", "sub"), None, "blocks"),
            P(("groups", "dp", "sub"), None, "blocks"),
            P("groups", None),
            P("groups", None),
            P("groups"),
            P("groups"),
        ),
        check_vma=False,
    )
```

```python
import functools

import jax
import jax.numpy as jnp
from jax import lax
from jax.experimental import pallas as pl
from jax.experimental.pallas import tpu as pltpu
from jax.sharding import PartitionSpec as P

C = 96
LANES = 128
SIDE = 8
KMAX = 2
LOW = 2
LEVELS = 4
EDGE = 2 * SIDE
PLANE = EDGE * EDGE
CELLS = LEVELS * PLANE
WIDE = EDGE * (EDGE + 2)
ROWS = 4 * SIDE * SIDE * KMAX
TAPS = 27
DEPTH = TAPS * LANES
TILES = 21
SUM_ROWS = 2048
BF16 = jnp.bfloat16
F32 = jnp.float32
MESH = pl.DeviceIdType.MESH


def side_offsets(parties):
    half = parties // 2
    found = []
    for offset in (1, parties - 1, (half + 1) % parties, (half - 1) % parties):
        if offset not in found:
            found.append(offset)
    return found


def stream_count(parties):
    return 2 if SUM_ROWS // 8 // parties % 16 == 0 else 1


def dot(left, right, dims=((1,), (0,))):
    return lax.dot_general(left, right, (dims, ((), ())), preferred_element_type=F32)


def slope_of(values):
    squash = jax.nn.sigmoid(values)
    return squash * (1.0 + values * (1.0 - squash))


def iota(shape, axis):
    return lax.broadcasted_iota(jnp.int32, shape, axis)


def one_hot(condition):
    return jnp.where(condition, 1.0, 0.0).astype(BF16)


def kernel(
    parties,
    *refs,
):
    given, refs = refs[:9], refs[9:]
    results, refs = refs[:6], refs[6:]
    held_in, refs = refs[:9], refs[9:]
    held_out, refs = refs[:6], refs[6:]
    (
        features,
        grad_out,
        weight_one,
        weight_two,
        bias_one,
        bias_two,
        heights,
        counts,
        neighbours,
    ) = held_in
    (
        out_features,
        input_grad,
        weight_one_grad,
        weight_two_grad,
        bias_one_grad,
        bias_two_grad,
    ) = held_out
    (
        place,
        spread_left,
        spread_right,
        pick,
        square,
        strided,
        taken_one,
        taken_two,
        bias_kept,
        back,
        taps_one,
        taps_two,
        taps_back,
        pre_kept,
        mask_kept,
        send_side,
        send_across,
        got_side,
        got_across,
        part,
        part_sent,
        got_core,
        core_sum,
        core_sent,
        got_chip,
        chip_sum,
        chip_sent,
        got_line,
        total,
        send_sem,
        recv_sem,
        sum_send,
        sum_recv,
        in_sem,
        out_sem,
    ) = refs

    def bring(number):
        return pltpu.make_async_copy(given[number], held_in[number], in_sem.at[number])

    def leave(number):
        return pltpu.make_async_copy(held_out[number], results[number], out_sem.at[number])

    for number in (6, 7, 8, 0, 2, 4, 5, 3, 1):
        bring(number).start()
    offsets = side_offsets(parties)
    half = parties // 2
    me = lax.axis_index("blocks")
    chip = lax.axis_index("dp")
    core = lax.axis_index("sub")
    streams = stream_count(parties)
    span = SUM_ROWS // streams
    share = span // 4 // parties
    partners = [{"blocks": lax.rem(me + offset, parties)} for offset in range(1, parties)]
    partners += [{"dp": 1 - chip}, {"sub": 1 - core}]

    barrier = pltpu.get_barrier_semaphore()
    for partner in partners:
        pl.semaphore_signal(barrier, inc=1, device_id=partner, device_id_type=MESH)

    for number in (6, 7, 8):
        bring(number).wait()
    lane = iota((SIDE * SIDE, LANES), 1)
    double = one_hot(lane // KMAX == iota((SIDE * SIDE, LANES), 0))
    low = dot(heights[0].astype(F32).astype(BF16), double).astype(jnp.int32)
    held = dot(counts[0].astype(F32).astype(BF16), double).astype(jnp.int32)
    lane = iota((1, LANES), 1)
    column = lane // KMAX
    layer = lane % KMAX
    cell_at = iota((CELLS, LANES), 0)
    for slot in range(4):
        cell = (SIDE * (slot // 2) + column // SIDE) * EDGE + SIDE * (slot % 2) + column % SIDE
        target = (low[slot : slot + 1] - LOW + layer) * PLANE + cell
        target = jnp.where(layer < held[slot : slot + 1], target, -1)
        place[:, slot * LANES : (slot + 1) * LANES] = one_hot(cell_at == target)
    mask_kept[...] = dot(place[...], jnp.ones((ROWS, LANES), BF16))

    row = iota((LEVELS * WIDE, LANES), 0)
    level = row // WIDE
    across = (row % WIDE) // EDGE
    along = row % EDGE
    wanted = jnp.where(
        across == 0,
        64 + level * EDGE + EDGE - 1,
        jnp.where(across == EDGE + 1, 64 + level * EDGE, level * EDGE + across - 1),
    )
    lane = iota((LEVELS * WIDE, LANES), 1)
    spread_left[...] = one_hot((along == 0) & (lane == wanted))
    spread_right[...] = one_hot((along == EDGE - 1) & (lane == wanted))
    number = iota((128, CELLS), 0)
    spot = (number % 64) * EDGE + jnp.where(number >= 64, EDGE - 1, 0)
    pick[...] = one_hot(iota((128, CELLS), 1) == spot)

    for taps in (taps_one, taps_two, taps_back):
        taps[0] = jnp.zeros((WIDE, 3 * LANES), BF16)
        taps[LEVELS + 1] = jnp.zeros((WIDE, 3 * LANES), BF16)

    for layer in range(2):
        spare = SUM_ROWS - TILES * C
        part[layer, TILES * C :] = jnp.zeros((spare, LANES), F32)
        part_sent[layer, TILES * C :] = jnp.zeros((spare, LANES), BF16)

    def dense(rows_ref):
        padded = jnp.concatenate([rows_ref[0], jnp.zeros((LANES - C, ROWS), BF16)], axis=0)
        return dot(place[...], padded, ((1,), (1,))).astype(BF16)

    def sparse(cells):
        return dot(jnp.transpose(cells), place[...])[:C].astype(BF16)

    def copies(turn):
        result = []
        for slot, offset in enumerate(offsets):
            result.append(
                pltpu.make_async_remote_copy(
                    src_ref=send_side.at[turn, slot],
                    dst_ref=got_side.at[turn, slot],
                    send_sem=send_sem.at[turn, slot],
                    recv_sem=recv_sem.at[turn, slot],
                    device_id={"blocks": lax.rem(me + offset, parties)},
                    device_id_type=MESH,
                )
            )
        result.append(
            pltpu.make_async_remote_copy(
                src_ref=send_across.at[turn],
                dst_ref=got_across.at[turn],
                send_sem=send_sem.at[turn, len(offsets)],
                recv_sem=recv_sem.at[turn, len(offsets)],
                device_id={"blocks": lax.rem(me + half, parties)},
                device_id_type=MESH,
            )
        )
        return result

    def send(turn, cells):
        both = dot(pick[...], cells)
        first, last = both[:64], both[64:]
        to_right = jnp.where(right, last, first).astype(BF16)
        to_left = jnp.where(left, first, last).astype(BF16)
        for slot, offset in enumerate(offsets):
            rightward = offset == 1 or (offset != parties - 1 and offset == half + 1)
            send_side[turn, slot] = to_right if rightward else to_left
        for z in range(LEVELS):
            first = cells[z * PLANE : z * PLANE + EDGE].astype(F32)
            last = cells[(z + 1) * PLANE - EDGE : (z + 1) * PLANE].astype(F32)
            chosen = jnp.where(up, first, last).astype(BF16)
            send_across[turn, z * EDGE : (z + 1) * EDGE] = chosen
        for copy in copies(turn):
            copy.start()

    def there(slot, direction):
        return jnp.broadcast_to(neighbours[0, slot : slot + 1, direction : direction + 1], (1, LANES)) >= 0

    up, down, left, right = there(0, 1), there(2, 0), there(0, 3), there(1, 2)

    def arrive(turn, cells, taps):
        for copy in copies(turn):
            copy.wait()
        inside = iota((64, LANES), 0) % EDGE
        corner = ((inside == EDGE - 1) & up) | ((inside == 0) & down)

        def columns(main, diagonal, there):
            straight = got_side[turn, offsets.index(main)]
            slanted = got_side[turn, offsets.index(diagonal)]
            both = jnp.concatenate(
                [
                    jnp.where(there, straight.astype(F32), 0.0),
                    jnp.where(corner & there, slanted.astype(F32), 0.0),
                ],
                axis=0,
            )
            return both.astype(BF16)

        from_left = columns(1, (half + 1) % parties, left)
        from_right = columns(parties - 1, (half - 1) % parties, right)
        pieces = []
        for z in range(LEVELS):
            beside = got_across[turn, z * EDGE : (z + 1) * EDGE].astype(F32)
            pieces.append(jnp.where(up, beside, 0.0))
            pieces.append(cells[z * PLANE : (z + 1) * PLANE].astype(F32))
            pieces.append(jnp.where(down, beside, 0.0))
        middle = jnp.concatenate(pieces, axis=0)
        place_along = iota((LEVELS * WIDE, LANES), 0) % EDGE
        before = jnp.where(place_along == 0, 0.0, pltpu.roll(middle, 1, 0))
        after = jnp.where(place_along == EDGE - 1, 0.0, pltpu.roll(middle, LEVELS * WIDE - 1, 0))
        before = (before + dot(spread_left[...], from_left)).astype(BF16)
        after = (after + dot(spread_right[...], from_right)).astype(BF16)
        middle = middle.astype(BF16)
        for z in range(LEVELS):
            part = slice(z * WIDE, (z + 1) * WIDE)
            taps[z + 1, :, 0:LANES] = before[part]
            taps[z + 1, :, LANES : 2 * LANES] = middle[part]
            taps[z + 1, :, 2 * LANES : 3 * LANES] = after[part]

    def convolve(taps, weights):
        results = []
        for z in range(LEVELS):
            parts = [
                taps[z + dz, dx * EDGE : dx * EDGE + PLANE] for dz in range(3) for dx in range(3)
            ]
            results.append(dot(jnp.concatenate(parts, axis=1), weights))
        return jnp.concatenate(results, axis=0)

    def weight_grad(gradient, taps, layer):
        flipped = jnp.transpose(gradient)
        for dz in range(3):
            for dx in range(3):
                field = jnp.concatenate(
                    [taps[z + dz, dx * EDGE : dx * EDGE + PLANE] for z in range(LEVELS)], axis=0
                )
                product = jnp.transpose(dot(flipped, field))
                for dy in range(3):
                    tap = (3 * dz + dx) * 3 + dy
                    strided[pl.ds(tap, C, stride=TAPS), :] = product[dy * LANES : dy * LANES + C]
        bias = jnp.sum(gradient.astype(F32), axis=0, keepdims=True)
        strided[TAPS * C :] = jnp.broadcast_to(bias, (C, LANES))
        for tile in range(TILES):
            piece = jnp.transpose(strided[tile * LANES : (tile + 1) * LANES])[:C]
            part[layer, tile * C : (tile + 1) * C] = piece
            part_sent[layer, tile * C : (tile + 1) * C] = piece.astype(BF16)

    half_rows, quarter = span // 2, span // 4

    def from_row(stream, row, length):
        first = pl.multiple_of((stream % streams) * span + row, 16)
        return stream // streams, pl.ds(first, length)

    mine = core * half_rows + chip * quarter

    def remote(source, landing, stream, number, partner):
        return pltpu.make_async_remote_copy(
            src_ref=source,
            dst_ref=landing,
            send_sem=sum_send.at[stream, number],
            recv_sem=sum_recv.at[stream, number],
            device_id=partner,
            device_id_type=MESH,
        )

    def over_cores(stream):
        other = from_row(stream, (1 - core) * half_rows, half_rows)
        return [
            remote(part_sent.at[other], got_core.at[stream], stream, 0, {"sub": 1 - core})
        ]

    def over_chips(stream):
        other = pl.ds(pl.multiple_of((1 - chip) * quarter, 16), quarter)
        return [
            remote(core_sent.at[stream, other], got_chip.at[stream], stream, 1, {"dp": 1 - chip})
        ]

    def over_line(stream):
        result = []
        for offset in range(1, parties):
            there = lax.rem(me + offset, parties)
            rows = pl.ds(pl.multiple_of(there * share, 16), share)
            result.append(
                remote(
                    chip_sent.at[stream, rows],
                    got_line.at[stream, offset - 1],
                    stream,
                    1 + offset,
                    {"blocks": there},
                )
            )
        return result

    def spread_line(stream):
        rows = total.at[from_row(stream, mine + me * share, share)]
        return [
            remote(rows, rows, stream, parties + offset, {"blocks": lax.rem(me + offset, parties)})
            for offset in range(1, parties)
        ]

    def spread_chips(stream):
        rows = total.at[from_row(stream, mine, quarter)]
        return [remote(rows, rows, stream, 2 * parties, {"dp": 1 - chip})]

    def spread_cores(stream):
        rows = total.at[from_row(stream, core * half_rows, half_rows)]
        return [remote(rows, rows, stream, 2 * parties + 1, {"sub": 1 - core})]

    def begin(copies_of, stream):
        for copy in copies_of(stream):
            copy.start()

    def finish(copies_of, stream):
        for copy in copies_of(stream):
            copy.wait()

    def sum_cores(stream):
        finish(over_cores, stream)
        own = part[from_row(stream, core * half_rows, half_rows)]
        value = own + got_core[stream].astype(F32)
        core_sum[stream] = value
        core_sent[stream] = value.astype(BF16)
        begin(over_chips, stream)

    def sum_chips(stream):
        finish(over_chips, stream)
        own = core_sum[stream, pl.ds(pl.multiple_of(chip * quarter, 16), quarter)]
        value = own + got_chip[stream].astype(F32)
        chip_sum[stream] = value
        chip_sent[stream] = value.astype(BF16)
        begin(over_line, stream)

    def sum_line(stream):
        finish(over_line, stream)
        value = chip_sum[stream, pl.ds(pl.multiple_of(me * share, 16), share)]
        for offset in range(1, parties):
            value = value + got_line[stream, offset - 1].astype(F32)
        value = value * (1.0 / (4 * parties))
        total[from_row(stream, mine + me * share, share)] = value.astype(BF16)
        begin(spread_line, stream)

    def take_taps(weights, taken):
        square[:C, : TAPS * C] = weights[...].astype(F32)
        for tile in range(TILES):
            part_of = slice(tile * LANES, (tile + 1) * LANES)
            strided[part_of] = jnp.transpose(square[:, part_of])
        for tap in range(TAPS):
            rows = strided[pl.ds(tap, C, stride=TAPS), :]
            taken[tap * LANES : tap * LANES + C] = rows.astype(BF16)
            taken[tap * LANES + C : (tap + 1) * LANES] = jnp.zeros((LANES - C, LANES), BF16)

    def turn_back(taken):
        for tap in range(TAPS):
            other = TAPS - 1 - tap
            tile = taken[other * LANES : (other + 1) * LANES]
            back[tap * LANES : (tap + 1) * LANES] = jnp.transpose(tile)

    def hand_out(layer, weights_out, bias_out):
        for tile in range(TILES - 1):
            piece = total[layer, tile * C : (tile + 1) * C]
            weights_out[:, tile * LANES : (tile + 1) * LANES] = piece.astype(F32)
        last = total[layer, (TILES - 1) * C :].astype(F32)
        rest = TAPS * C - (TILES - 1) * LANES
        weights_out[:, (TILES - 1) * LANES :] = last[:C, :rest]
        bias_out[...] = jnp.transpose(last)[rest : rest + 1, :C]

    square[...] = jnp.zeros((LANES, TILES * LANES), F32)
    bias_kept[...] = jnp.zeros((2, 1, LANES), F32)
    for number in (4, 5, 0):
        bring(number).wait()
    bias_kept[0, :, :C] = bias_one[...]
    bias_kept[1, :, :C] = bias_two[...]
    live = mask_kept[...] > 0
    cells = dense(features)
    pl.semaphore_wait(barrier, len(partners))
    send(0, cells)
    bring(2).wait()
    take_taps(weight_one, taken_one)
    arrive(0, cells, taps_one)

    pre_one = convolve(taps_one, taken_one[...]) + bias_kept[0]
    pre_kept[...] = pre_one
    hidden = jnp.where(live, pre_one * jax.nn.sigmoid(pre_one), 0.0).astype(BF16)
    send(1, hidden)
    bring(3).wait()
    take_taps(weight_two, taken_two)
    bring(1).wait()
    upstream = dense(grad_out)
    turn_back(taken_two)
    arrive(1, hidden, taps_two)

    pre_two = convolve(taps_two, taken_two[...]) + bias_kept[1]
    grad_two = jnp.where(live, upstream.astype(F32) * slope_of(pre_two), 0.0).astype(BF16)
    send(2, grad_two)
    activated = jnp.where(live, pre_two * jax.nn.sigmoid(pre_two), 0.0).astype(BF16)
    out_features[0] = sparse(activated)
    leave(0).start()
    weight_grad(grad_two, taps_two, 0)
    second, first = range(streams), range(streams, 2 * streams)
    for stream in second:
        begin(over_cores, stream)
    arrive(2, grad_two, taps_back)
    for stream in second:
        sum_cores(stream)

    hidden_sum = convolve(taps_back, back[...])
    grad_one = jnp.where(live, hidden_sum * slope_of(pre_kept[...]), 0.0).astype(BF16)
    send(3, grad_one)
    for stream in second:
        sum_chips(stream)
    turn_back(taken_one)
    weight_grad(grad_one, taps_one, 1)
    for stream in first:
        begin(over_cores, stream)
    for stream in second:
        sum_line(stream)
    for stream in first:
        sum_cores(stream)
    arrive(3, grad_one, taps_back)
    for stream in second:
        finish(spread_line, stream)
        begin(spread_chips, stream)
    for stream in first:
        sum_chips(stream)
    result = convolve(taps_back, back[...]).astype(BF16)
    for stream in second:
        finish(spread_chips, stream)
        begin(spread_cores, stream)
    for stream in first:
        sum_line(stream)
    input_grad[0] = sparse(result)
    leave(1).start()
    for stream in first:
        finish(spread_line, stream)
        begin(spread_chips, stream)
    for stream in second:
        finish(spread_cores, stream)
    hand_out(0, weight_two_grad, bias_two_grad)
    leave(3).start()
    leave(5).start()
    for stream in first:
        finish(spread_chips, stream)
        begin(spread_cores, stream)
    for stream in first:
        finish(spread_cores, stream)
    hand_out(1, weight_one_grad, bias_one_grad)
    leave(2).start()
    leave(4).start()
    for number in range(6):
        leave(number).wait()


def on_device(
    features, grad_out, weight_one, weight_two, bias_one, bias_two, heights, counts, neighbours
):
    parties = lax.axis_size("blocks")
    sides = len(side_offsets(parties))
    streams = stream_count(parties)
    span = SUM_ROWS // streams
    anywhere = pl.BlockSpec(memory_space=pl.ANY)
    given = (
        features,
        grad_out,
        weight_one,
        weight_two,
        bias_one[None],
        bias_two[None],
        heights,
        counts,
        neighbours,
    )
    out_shape = (
        jax.ShapeDtypeStruct((1, C, ROWS), BF16),
        jax.ShapeDtypeStruct((1, C, ROWS), BF16),
        jax.ShapeDtypeStruct((C, TAPS * C), F32),
        jax.ShapeDtypeStruct((C, TAPS * C), F32),
        jax.ShapeDtypeStruct((1, C), F32),
        jax.ShapeDtypeStruct((1, C), F32),
    )
    results = pl.pallas_call(
        functools.partial(kernel, parties),
        out_shape=out_shape,
        in_specs=[anywhere] * 9,
        out_specs=[anywhere] * 6,
        scratch_shapes=[pltpu.VMEM(array.shape, array.dtype) for array in given + out_shape]
        + [
            pltpu.VMEM((CELLS, ROWS), BF16),
            pltpu.VMEM((LEVELS * WIDE, LANES), BF16),
            pltpu.VMEM((LEVELS * WIDE, LANES), BF16),
            pltpu.VMEM((128, CELLS), BF16),
            pltpu.VMEM((LANES, TILES * LANES), F32),
            pltpu.VMEM((TILES * LANES, LANES), F32),
            pltpu.VMEM((DEPTH, LANES), BF16),
            pltpu.VMEM((DEPTH, LANES), BF16),
            pltpu.VMEM((2, 1, LANES), F32),
            pltpu.VMEM((DEPTH, LANES), BF16),
            pltpu.VMEM((LEVELS + 2, WIDE, 3 * LANES), BF16),
            pltpu.VMEM((LEVELS + 2, WIDE, 3 * LANES), BF16),
            pltpu.VMEM((LEVELS + 2, WIDE, 3 * LANES), BF16),
            pltpu.VMEM((CELLS, LANES), F32),
            pltpu.VMEM((CELLS, LANES), F32),
            pltpu.VMEM((4, sides, 64, LANES), BF16),
            pltpu.VMEM((4, 64, LANES), BF16),
            pltpu.VMEM((4, sides, 64, LANES), BF16),
            pltpu.VMEM((4, 64, LANES), BF16),
            pltpu.VMEM((2, SUM_ROWS, LANES), F32),
            pltpu.VMEM((2, SUM_ROWS, LANES), BF16),
            pltpu.VMEM((2 * streams, span // 2, LANES), BF16),
            pltpu.VMEM((2 * streams, span // 2, LANES), F32),
            pltpu.VMEM((2 * streams, span // 2, LANES), BF16),
            pltpu.VMEM((2 * streams, span // 4, LANES), BF16),
            pltpu.VMEM((2 * streams, span // 4, LANES), F32),
            pltpu.VMEM((2 * streams, span // 4, LANES), BF16),
            pltpu.VMEM((2 * streams, parties - 1, span // 4 // parties, LANES), BF16),
            pltpu.VMEM((2, SUM_ROWS, LANES), BF16),
            pltpu.SemaphoreType.DMA((4, sides + 1)),
            pltpu.SemaphoreType.DMA((4, sides + 1)),
            pltpu.SemaphoreType.DMA((2 * streams, 2 * parties + 2)),
            pltpu.SemaphoreType.DMA((2 * streams, 2 * parties + 2)),
            pltpu.SemaphoreType.DMA((9,)),
            pltpu.SemaphoreType.DMA((6,)),
        ],
        compiler_params=pltpu.CompilerParams(
            collective_id=0, has_side_effects=True, vmem_limit_bytes=60 * 1024 * 1024
        ),
    )(*given)
    return (*results[:4], results[4][0], results[5][0])


def solution(mesh):
    placed = (
        P(("groups", "dp", "sub"), None, "blocks"),
        P(("groups", "dp", "sub"), None, "blocks"),
        P(),
        P(),
        P(),
        P(),
        P(("groups", "dp", "sub"), "blocks", None),
        P(("groups", "dp", "sub"), "blocks", None),
        P(("groups", "dp", "sub"), "blocks", None),
    )
    return jax.shard_map(
        on_device,
        mesh=mesh,
        in_specs=placed,
        out_specs=(
            P(("groups", "dp", "sub"), None, "blocks"),
            P(("groups", "dp", "sub"), None, "blocks"),
            P("groups", None),
            P("groups", None),
            P("groups"),
            P("groups"),
        ),
        check_vma=False,
    )
```

```python
import functools

import jax
import jax.numpy as jnp
from jax import lax
from jax.experimental import pallas as pl
from jax.experimental.pallas import tpu as pltpu
from jax.sharding import PartitionSpec as P

C = 96
LANES = 128
SIDE = 8
KMAX = 2
LOW = 2
LEVELS = 4
EDGE = 2 * SIDE
PLANE = EDGE * EDGE
CELLS = LEVELS * PLANE
WIDE = EDGE * (EDGE + 2)
ROWS = 4 * SIDE * SIDE * KMAX
TAPS = 27
DEPTH = TAPS * LANES
TILES = 21
SUM_ROWS = 2048
BF16 = jnp.bfloat16
F32 = jnp.float32
MESH = pl.DeviceIdType.MESH


def side_offsets(parties):
    half = parties // 2
    found = []
    for offset in (1, parties - 1, (half + 1) % parties, (half - 1) % parties):
        if offset not in found:
            found.append(offset)
    return found


def stream_count(parties):
    return 2 if SUM_ROWS // 8 // parties % 16 == 0 else 1


def dot(left, right, dims=((1,), (0,))):
    return lax.dot_general(left, right, (dims, ((), ())), preferred_element_type=F32)


def slope_of(values):
    squash = jax.nn.sigmoid(values)
    return squash * (1.0 + values * (1.0 - squash))


def iota(shape, axis):
    return lax.broadcasted_iota(jnp.int32, shape, axis)


def one_hot(condition):
    return jnp.where(condition, 1.0, 0.0).astype(BF16)


def kernel(
    parties,
    *refs,
):
    given, refs = refs[:9], refs[9:]
    results, refs = refs[:6], refs[6:]
    held_in, refs = refs[:9], refs[9:]
    (
        features,
        grad_out,
        weight_one,
        weight_two,
        bias_one,
        bias_two,
        heights,
        counts,
        neighbours,
    ) = held_in
    (
        out_features,
        input_grad,
        weight_one_grad,
        weight_two_grad,
        bias_one_grad,
        bias_two_grad,
    ) = results
    (
        place,
        spread_left,
        spread_right,
        pick,
        square,
        strided,
        taken_one,
        taken_two,
        bias_kept,
        back,
        taps_one,
        taps_two,
        taps_back,
        pre_kept,
        mask_kept,
        send_side,
        send_across,
        got_side,
        got_across,
        part,
        part_sent,
        got_core,
        core_sum,
        core_sent,
        got_chip,
        chip_sum,
        chip_sent,
        got_line,
        total,
        send_sem,
        recv_sem,
        sum_send,
        sum_recv,
        in_sem,
    ) = refs

    def bring(number):
        return pltpu.make_async_copy(given[number], held_in[number], in_sem.at[number])

    for number in (6, 7, 8, 0, 2, 4, 5, 3, 1):
        bring(number).start()
    offsets = side_offsets(parties)
    half = parties // 2
    me = lax.axis_index("blocks")
    chip = lax.axis_index("dp")
    core = lax.axis_index("sub")
    streams = stream_count(parties)
    span = SUM_ROWS // streams
    share = span // 4 // parties
    partners = [{"blocks": lax.rem(me + offset, parties)} for offset in range(1, parties)]
    partners += [{"dp": 1 - chip}, {"sub": 1 - core}]

    barrier = pltpu.get_barrier_semaphore()
    for partner in partners:
        pl.semaphore_signal(barrier, inc=1, device_id=partner, device_id_type=MESH)

    for number in (6, 7, 8):
        bring(number).wait()
    lane = iota((SIDE * SIDE, LANES), 1)
    double = one_hot(lane // KMAX == iota((SIDE * SIDE, LANES), 0))
    low = dot(heights[0].astype(F32).astype(BF16), double).astype(jnp.int32)
    held = dot(counts[0].astype(F32).astype(BF16), double).astype(jnp.int32)
    lane = iota((1, LANES), 1)
    column = lane // KMAX
    layer = lane % KMAX
    cell_at = iota((CELLS, LANES), 0)
    for slot in range(4):
        cell = (SIDE * (slot // 2) + column // SIDE) * EDGE + SIDE * (slot % 2) + column % SIDE
        target = (low[slot : slot + 1] - LOW + layer) * PLANE + cell
        target = jnp.where(layer < held[slot : slot + 1], target, -1)
        place[:, slot * LANES : (slot + 1) * LANES] = one_hot(cell_at == target)
    number = iota((128, CELLS), 0)
    spot = (number % 64) * EDGE + jnp.where(number >= 64, EDGE - 1, 0)
    pick[...] = one_hot(iota((128, CELLS), 1) == spot)

    def dense(rows_ref):
        padded = jnp.concatenate([rows_ref[0], jnp.zeros((LANES - C, ROWS), BF16)], axis=0)
        return dot(place[...], padded, ((1,), (1,))).astype(BF16)

    def sparse(cells):
        return dot(jnp.transpose(cells), place[...])[:C].astype(BF16)

    def copies(turn):
        result = []
        for slot, offset in enumerate(offsets):
            result.append(
                pltpu.make_async_remote_copy(
                    src_ref=send_side.at[turn, slot],
                    dst_ref=got_side.at[turn, slot],
                    send_sem=send_sem.at[turn, slot],
                    recv_sem=recv_sem.at[turn, slot],
                    device_id={"blocks": lax.rem(me + offset, parties)},
                    device_id_type=MESH,
                )
            )
        result.append(
            pltpu.make_async_remote_copy(
                src_ref=send_across.at[turn],
                dst_ref=got_across.at[turn],
                send_sem=send_sem.at[turn, len(offsets)],
                recv_sem=recv_sem.at[turn, len(offsets)],
                device_id={"blocks": lax.rem(me + half, parties)},
                device_id_type=MESH,
            )
        )
        return result

    def send(turn, cells):
        both = dot(pick[...], cells)
        first, last = both[:64], both[64:]
        to_right = jnp.where(right, last, first).astype(BF16)
        to_left = jnp.where(left, first, last).astype(BF16)
        for slot, offset in enumerate(offsets):
            rightward = offset == 1 or (offset != parties - 1 and offset == half + 1)
            send_side[turn, slot] = to_right if rightward else to_left
        for z in range(LEVELS):
            first = cells[z * PLANE : z * PLANE + EDGE].astype(F32)
            last = cells[(z + 1) * PLANE - EDGE : (z + 1) * PLANE].astype(F32)
            chosen = jnp.where(up, first, last).astype(BF16)
            send_across[turn, z * EDGE : (z + 1) * EDGE] = chosen
        for copy in copies(turn):
            copy.start()

    def there(slot, direction):
        return jnp.broadcast_to(neighbours[0, slot : slot + 1, direction : direction + 1], (1, LANES)) >= 0

    up, down, left, right = there(0, 1), there(2, 0), there(0, 3), there(1, 2)

    def arrive(turn, cells, taps):
        along = iota((PLANE, LANES), 0) % EDGE

        def shifted(values):
            rows = values.shape[0]
            at = along[:rows]
            return (
                jnp.where(at == 0, 0.0, pltpu.roll(values, 1, 0)),
                values,
                jnp.where(at == EDGE - 1, 0.0, pltpu.roll(values, rows - 1, 0)),
            )

        own = [shifted(cells[z * PLANE : (z + 1) * PLANE].astype(F32)) for z in range(LEVELS)]
        for copy in copies(turn):
            copy.wait()
        inside = iota((64, LANES), 0) % EDGE
        corner = ((inside == EDGE - 1) & up) | ((inside == 0) & down)

        def columns(main, diagonal, there):
            straight = got_side[turn, offsets.index(main)]
            slanted = got_side[turn, offsets.index(diagonal)]
            both = jnp.concatenate(
                [
                    jnp.where(there, straight.astype(F32), 0.0),
                    jnp.where(corner & there, slanted.astype(F32), 0.0),
                ],
                axis=0,
            )
            return both.astype(BF16)

        from_left = columns(1, (half + 1) % parties, left)
        from_right = columns(parties - 1, (half - 1) % parties, right)
        pieces = [[], [], []]
        for z in range(LEVELS):
            beside = shifted(got_across[turn, z * EDGE : (z + 1) * EDGE].astype(F32))
            for part, outer, inner in zip(pieces, beside, own[z]):
                part += [jnp.where(up, outer, 0.0), inner, jnp.where(down, outer, 0.0)]
        before, middle, after = [jnp.concatenate(part, axis=0) for part in pieces]
        before = (before + dot(spread_left[...], from_left)).astype(BF16)
        after = (after + dot(spread_right[...], from_right)).astype(BF16)
        middle = middle.astype(BF16)
        for z in range(LEVELS):
            part = slice(z * WIDE, (z + 1) * WIDE)
            taps[z + 1, :, 0:LANES] = before[part]
            taps[z + 1, :, LANES : 2 * LANES] = middle[part]
            taps[z + 1, :, 2 * LANES : 3 * LANES] = after[part]

    def convolve(taps, weights):
        results = []
        for z in range(LEVELS):
            parts = [
                taps[z + dz, dx * EDGE : dx * EDGE + PLANE] for dz in range(3) for dx in range(3)
            ]
            results.append(dot(jnp.concatenate(parts, axis=1), weights))
        return jnp.concatenate(results, axis=0)

    def weight_grad(gradient, taps, layer):
        flipped = jnp.transpose(gradient)
        for dz in range(3):
            for dx in range(3):
                field = jnp.concatenate(
                    [taps[z + dz, dx * EDGE : dx * EDGE + PLANE] for z in range(LEVELS)], axis=0
                )
                product = jnp.transpose(dot(flipped, field))
                for dy in range(3):
                    tap = (3 * dz + dx) * 3 + dy
                    strided[pl.ds(tap, C, stride=TAPS), :] = product[dy * LANES : dy * LANES + C]
        bias = jnp.sum(gradient.astype(F32), axis=0, keepdims=True)
        strided[TAPS * C :] = jnp.broadcast_to(bias, (C, LANES))
        for tile in range(TILES):
            piece = jnp.transpose(strided[tile * LANES : (tile + 1) * LANES])[:C]
            part[layer, tile * C : (tile + 1) * C] = piece
            part_sent[layer, tile * C : (tile + 1) * C] = piece.astype(BF16)

    half_rows, quarter = span // 2, span // 4

    def from_row(stream, row, length):
        first = pl.multiple_of((stream % streams) * span + row, 16)
        return stream // streams, pl.ds(first, length)

    mine = core * half_rows + chip * quarter

    def remote(source, landing, stream, number, partner):
        return pltpu.make_async_remote_copy(
            src_ref=source,
            dst_ref=landing,
            send_sem=sum_send.at[stream, number],
            recv_sem=sum_recv.at[stream, number],
            device_id=partner,
            device_id_type=MESH,
        )

    def over_cores(stream):
        other = from_row(stream, (1 - core) * half_rows, half_rows)
        return [
            remote(part_sent.at[other], got_core.at[stream], stream, 0, {"sub": 1 - core})
        ]

    def over_chips(stream):
        other = pl.ds(pl.multiple_of((1 - chip) * quarter, 16), quarter)
        return [
            remote(core_sent.at[stream, other], got_chip.at[stream], stream, 1, {"dp": 1 - chip})
        ]

    def over_line(stream):
        result = []
        for offset in range(1, parties):
            there = lax.rem(me + offset, parties)
            rows = pl.ds(pl.multiple_of(there * share, 16), share)
            result.append(
                remote(
                    chip_sent.at[stream, rows],
                    got_line.at[stream, offset - 1],
                    stream,
                    1 + offset,
                    {"blocks": there},
                )
            )
        return result

    def spread_line(stream):
        rows = total.at[from_row(stream, mine + me * share, share)]
        return [
            remote(rows, rows, stream, parties + offset, {"blocks": lax.rem(me + offset, parties)})
            for offset in range(1, parties)
        ]

    def spread_chips(stream):
        rows = total.at[from_row(stream, mine, quarter)]
        return [remote(rows, rows, stream, 2 * parties, {"dp": 1 - chip})]

    def spread_cores(stream):
        rows = total.at[from_row(stream, core * half_rows, half_rows)]
        return [remote(rows, rows, stream, 2 * parties + 1, {"sub": 1 - core})]

    def begin(copies_of, stream):
        for copy in copies_of(stream):
            copy.start()

    def finish(copies_of, stream):
        for copy in copies_of(stream):
            copy.wait()

    def sum_cores(stream):
        finish(over_cores, stream)
        own = part[from_row(stream, core * half_rows, half_rows)]
        value = own + got_core[stream].astype(F32)
        core_sum[stream] = value
        core_sent[stream] = value.astype(BF16)
        begin(over_chips, stream)

    def sum_chips(stream):
        finish(over_chips, stream)
        own = core_sum[stream, pl.ds(pl.multiple_of(chip * quarter, 16), quarter)]
        value = own + got_chip[stream].astype(F32)
        chip_sum[stream] = value
        chip_sent[stream] = value.astype(BF16)
        begin(over_line, stream)

    def sum_line(stream):
        finish(over_line, stream)
        value = chip_sum[stream, pl.ds(pl.multiple_of(me * share, 16), share)]
        for offset in range(1, parties):
            value = value + got_line[stream, offset - 1].astype(F32)
        value = value * (1.0 / (4 * parties))
        total[from_row(stream, mine + me * share, share)] = value.astype(BF16)
        begin(spread_line, stream)

    def take_taps(weights, taken):
        square[:C, : TAPS * C] = weights[...].astype(F32)
        for tile in range(TILES):
            part_of = slice(tile * LANES, (tile + 1) * LANES)
            strided[part_of] = jnp.transpose(square[:, part_of])
        for tap in range(TAPS):
            rows = strided[pl.ds(tap, C, stride=TAPS), :]
            taken[tap * LANES : tap * LANES + C] = rows.astype(BF16)
            taken[tap * LANES + C : (tap + 1) * LANES] = jnp.zeros((LANES - C, LANES), BF16)

    def turn_back(taken):
        for tap in range(TAPS):
            other = TAPS - 1 - tap
            tile = taken[other * LANES : (other + 1) * LANES]
            back[tap * LANES : (tap + 1) * LANES] = jnp.transpose(tile)

    def hand_out(layer, weights_out, bias_out):
        for tile in range(TILES - 1):
            piece = total[layer, tile * C : (tile + 1) * C]
            weights_out[:, tile * LANES : (tile + 1) * LANES] = piece.astype(F32)
        last = total[layer, (TILES - 1) * C :].astype(F32)
        rest = TAPS * C - (TILES - 1) * LANES
        weights_out[:, (TILES - 1) * LANES :] = last[:C, :rest]
        bias_out[...] = jnp.transpose(last)[rest : rest + 1, :C]

    bring(0).wait()
    cells = dense(features)
    pl.semaphore_wait(barrier, len(partners))
    send(0, cells)
    mask_kept[...] = dot(place[...], jnp.ones((ROWS, LANES), BF16))
    live = mask_kept[...] > 0
    row = iota((LEVELS * WIDE, LANES), 0)
    level = row // WIDE
    across = (row % WIDE) // EDGE
    along = row % EDGE
    wanted = jnp.where(
        across == 0,
        64 + level * EDGE + EDGE - 1,
        jnp.where(across == EDGE + 1, 64 + level * EDGE, level * EDGE + across - 1),
    )
    lane = iota((LEVELS * WIDE, LANES), 1)
    spread_left[...] = one_hot((along == 0) & (lane == wanted))
    spread_right[...] = one_hot((along == EDGE - 1) & (lane == wanted))
    for taps in (taps_one, taps_two, taps_back):
        taps[0] = jnp.zeros((WIDE, 3 * LANES), BF16)
        taps[LEVELS + 1] = jnp.zeros((WIDE, 3 * LANES), BF16)

    for layer in range(2):
        spare = SUM_ROWS - TILES * C
        part[layer, TILES * C :] = jnp.zeros((spare, LANES), F32)
        part_sent[layer, TILES * C :] = jnp.zeros((spare, LANES), BF16)
    square[...] = jnp.zeros((LANES, TILES * LANES), F32)
    bias_kept[...] = jnp.zeros((2, 1, LANES), F32)
    for number in (4, 5):
        bring(number).wait()
    bias_kept[0, :, :C] = bias_one[...]
    bias_kept[1, :, :C] = bias_two[...]
    bring(2).wait()
    take_taps(weight_one, taken_one)
    arrive(0, cells, taps_one)

    pre_one = convolve(taps_one, taken_one[...]) + bias_kept[0]
    pre_kept[...] = pre_one
    hidden = jnp.where(live, pre_one * jax.nn.sigmoid(pre_one), 0.0).astype(BF16)
    send(1, hidden)
    bring(3).wait()
    take_taps(weight_two, taken_two)
    bring(1).wait()
    upstream = dense(grad_out)
    turn_back(taken_two)
    arrive(1, hidden, taps_two)

    pre_two = convolve(taps_two, taken_two[...]) + bias_kept[1]
    grad_two = jnp.where(live, upstream.astype(F32) * slope_of(pre_two), 0.0).astype(BF16)
    send(2, grad_two)
    activated = jnp.where(live, pre_two * jax.nn.sigmoid(pre_two), 0.0).astype(BF16)
    out_features[0] = sparse(activated)
    weight_grad(grad_two, taps_two, 0)
    second, first = range(streams), range(streams, 2 * streams)
    for stream in second:
        begin(over_cores, stream)
    arrive(2, grad_two, taps_back)
    for stream in second:
        sum_cores(stream)

    hidden_sum = convolve(taps_back, back[...])
    grad_one = jnp.where(live, hidden_sum * slope_of(pre_kept[...]), 0.0).astype(BF16)
    send(3, grad_one)
    for stream in second:
        sum_chips(stream)
    turn_back(taken_one)
    weight_grad(grad_one, taps_one, 1)
    for stream in first:
        begin(over_cores, stream)
    for stream in second:
        sum_line(stream)
    for stream in first:
        sum_cores(stream)
    arrive(3, grad_one, taps_back)
    for stream in second:
        finish(spread_line, stream)
        begin(spread_chips, stream)
    for stream in first:
        sum_chips(stream)
    result = convolve(taps_back, back[...]).astype(BF16)
    for stream in second:
        finish(spread_chips, stream)
        begin(spread_cores, stream)
    for stream in first:
        sum_line(stream)
    input_grad[0] = sparse(result)
    for stream in first:
        finish(spread_line, stream)
        begin(spread_chips, stream)
    for stream in second:
        finish(spread_cores, stream)
    hand_out(0, weight_two_grad, bias_two_grad)
    for stream in first:
        finish(spread_chips, stream)
        begin(spread_cores, stream)
    for stream in first:
        finish(spread_cores, stream)
    hand_out(1, weight_one_grad, bias_one_grad)


def on_device(
    features, grad_out, weight_one, weight_two, bias_one, bias_two, heights, counts, neighbours
):
    parties = lax.axis_size("blocks")
    sides = len(side_offsets(parties))
    streams = stream_count(parties)
    span = SUM_ROWS // streams
    anywhere = pl.BlockSpec(memory_space=pl.ANY)
    given = (
        features,
        grad_out,
        weight_one,
        weight_two,
        bias_one[None],
        bias_two[None],
        heights,
        counts,
        neighbours,
    )
    out_shape = (
        jax.ShapeDtypeStruct((1, C, ROWS), BF16),
        jax.ShapeDtypeStruct((1, C, ROWS), BF16),
        jax.ShapeDtypeStruct((C, TAPS * C), F32),
        jax.ShapeDtypeStruct((C, TAPS * C), F32),
        jax.ShapeDtypeStruct((1, C), F32),
        jax.ShapeDtypeStruct((1, C), F32),
    )
    results = pl.pallas_call(
        functools.partial(kernel, parties),
        out_shape=out_shape,
        in_specs=[anywhere] * 9,
        out_specs=[pl.BlockSpec(memory_space=pltpu.VMEM)] * 6,
        scratch_shapes=[pltpu.VMEM(array.shape, array.dtype) for array in given]
        + [
            pltpu.VMEM((CELLS, ROWS), BF16),
            pltpu.VMEM((LEVELS * WIDE, LANES), BF16),
            pltpu.VMEM((LEVELS * WIDE, LANES), BF16),
            pltpu.VMEM((128, CELLS), BF16),
            pltpu.VMEM((LANES, TILES * LANES), F32),
            pltpu.VMEM((TILES * LANES, LANES), F32),
            pltpu.VMEM((DEPTH, LANES), BF16),
            pltpu.VMEM((DEPTH, LANES), BF16),
            pltpu.VMEM((2, 1, LANES), F32),
            pltpu.VMEM((DEPTH, LANES), BF16),
            pltpu.VMEM((LEVELS + 2, WIDE, 3 * LANES), BF16),
            pltpu.VMEM((LEVELS + 2, WIDE, 3 * LANES), BF16),
            pltpu.VMEM((LEVELS + 2, WIDE, 3 * LANES), BF16),
            pltpu.VMEM((CELLS, LANES), F32),
            pltpu.VMEM((CELLS, LANES), F32),
            pltpu.VMEM((4, sides, 64, LANES), BF16),
            pltpu.VMEM((4, 64, LANES), BF16),
            pltpu.VMEM((4, sides, 64, LANES), BF16),
            pltpu.VMEM((4, 64, LANES), BF16),
            pltpu.VMEM((2, SUM_ROWS, LANES), F32),
            pltpu.VMEM((2, SUM_ROWS, LANES), BF16),
            pltpu.VMEM((2 * streams, span // 2, LANES), BF16),
            pltpu.VMEM((2 * streams, span // 2, LANES), F32),
            pltpu.VMEM((2 * streams, span // 2, LANES), BF16),
            pltpu.VMEM((2 * streams, span // 4, LANES), BF16),
            pltpu.VMEM((2 * streams, span // 4, LANES), F32),
            pltpu.VMEM((2 * streams, span // 4, LANES), BF16),
            pltpu.VMEM((2 * streams, parties - 1, span // 4 // parties, LANES), BF16),
            pltpu.VMEM((2, SUM_ROWS, LANES), BF16),
            pltpu.SemaphoreType.DMA((4, sides + 1)),
            pltpu.SemaphoreType.DMA((4, sides + 1)),
            pltpu.SemaphoreType.DMA((2 * streams, 2 * parties + 2)),
            pltpu.SemaphoreType.DMA((2 * streams, 2 * parties + 2)),
            pltpu.SemaphoreType.DMA((9,)),
        ],
        compiler_params=pltpu.CompilerParams(
            collective_id=0, has_side_effects=True, vmem_limit_bytes=60 * 1024 * 1024
        ),
    )(*given)
    return (*results[:4], results[4][0], results[5][0])


def solution(mesh):
    placed = (
        P(("groups", "dp", "sub"), None, "blocks"),
        P(("groups", "dp", "sub"), None, "blocks"),
        P(),
        P(),
        P(),
        P(),
        P(("groups", "dp", "sub"), "blocks", None),
        P(("groups", "dp", "sub"), "blocks", None),
        P(("groups", "dp", "sub"), "blocks", None),
    )
    return jax.shard_map(
        on_device,
        mesh=mesh,
        in_specs=placed,
        out_specs=(
            P(("groups", "dp", "sub"), None, "blocks"),
            P(("groups", "dp", "sub"), None, "blocks"),
            P("groups", None),
            P("groups", None),
            P("groups"),
            P("groups"),
        ),
        check_vma=False,
    )
```
